32 devices in a mesh: fsdp: 4 (over x, core), ctx: 2 (over y), tp: 4 (over z).
Axes of the slice: x: 2, y: 2, z: 4, core: 2. Of those that a mesh axis runs over, the one named last changes fastest.
Arguments:
- hidden_in: bfloat16 [4, 1408, 2048], P('fsdp', 'ctx'), may hold values from -6 to 6
- doc_lengths: int32 [4, 4], P('fsdp'), may hold values from 1 to 1024, 1408 in all within a row
- expert_ids: int32 [4, 1408, 4], P('fsdp', 'ctx'), may hold values from 0 to 7, all different within a row
- fill_rank: int32 [4, 2, 704], P('fsdp', 'ctx'), may hold values from 0 to 703, each once within a row
- norm_gains: bfloat16 [2, 2048], replicated, may hold values from 0.5 to 1.5
- qkv_weight: bfloat16 [2048, 3, 2048], P(('fsdp', 'ctx'), None, 'tp'), may hold values from -0.125 to 0.125
- qkv_bias: bfloat16 [3, 2048], P(None, 'tp'), may hold values from -1 to 1
- out_weight: bfloat16 [2048, 2048], P('tp', ('fsdp', 'ctx')), may hold values from -2 to 2
- router_weight: bfloat16 [2048, 8], replicated, may hold values from -0.0625 to 0.0625
- blend_weight: bfloat16 [2048], replicated, may hold values from -0.125 to 0.125
- shared_inner: bfloat16 [2048, 2, 5632], P(('fsdp', 'ctx'), None, 'tp'), may hold values from -0.125 to 0.125
- shared_outer: bfloat16 [5632, 2048], P('tp', ('fsdp', 'ctx')), may hold values from -0.15625 to 0.15625
- expert_inner: bfloat16 [8, 2048, 2, 1408], P(('fsdp', 'ctx'), None, None, 'tp'), may hold values from -0.125 to 0.125
- expert_outer: bfloat16 [8, 1408, 2048], P(('fsdp', 'ctx'), 'tp'), may hold values from -0.4375 to 0.4375
- cotangent: bfloat16 [4, 1408, 2048], P('fsdp', 'ctx'), may hold values from -6 to 6
Outputs:
- layer_out: bfloat16 [4, 1408, 2048], P('fsdp', 'ctx')
- input_grad: bfloat16 [4, 1408, 2048], P('fsdp', 'ctx')
- gains_grad: float32 [2, 2048], replicated
- qkv_grad: float32 [2048, 3, 2048], P(('fsdp', 'ctx'), None, 'tp')
- bias_grad: float32 [3, 2048], P(None, 'tp')
- projection_grad: float32 [2048, 2048], P('tp', ('fsdp', 'ctx'))
- router_grad: float32 [2048, 8], replicated
- blend_grad: float32 [2048], replicated
- inner_shared: float32 [2048, 2, 5632], P(('fsdp', 'ctx'), None, 'tp')
- outer_shared: float32 [5632, 2048], P('tp', ('fsdp', 'ctx'))
- inner_expert: float32 [8, 2048, 2, 1408], P(('fsdp', 'ctx'), None, None, 'tp')
- outer_expert: float32 [8, 1408, 2048], P(('fsdp', 'ctx'), 'tp')
The draws below stay inside these ranges and needn't reach their ends.
Inputs may be any that keep to these rules, and one draw needn't show every extreme that they name: `doc_lengths`: in each sequence the 4 lengths add up to 1408 and the longest is exactly 1024. `expert_ids`: each token names 4 different experts. `fill_rank`: for each index of fsdp and ctx, the 704 priorities of its block (its sequences' positions in order) are a permutation; a lower priority takes a slot first.
All inputs are finite; a program needn't handle non-finite values.
Results may differ from the reference program's by a relative error of at most 0.022.
Values may be sent and summed in bfloat16 or wider, within the bound.
No kernel may reach another device: no remote copies, remote signals or barrier semaphores. Data moves between devices by JAX's collectives and lax.ppermute only.
A program may use at most 384 MiB of HBM per device.

```python
import math
import jax
import jax.numpy as jnp
import numpy as np
from jax import lax

MODEL_WIDTH = 2048
HEADS = 16
HEAD_DIM = 128
FS = 5632
FE = 1408
TOP = 4
SEQUENCE_LENGTH = 1408
SEQS = 1
WINDOW = 1024
DOCS = 4
DOC_MOST = 1024
EXPERTS = 8
SEQUENCE_TOTAL = 4
HALF = 704
TOK_DEV = 704
CAP = 352
N_FSDP = 4
N_CTX = 2


def with_spikes(array, stream_key, source, target, parts, factor):
    def block_of(dim):
        return (jnp.arange(array.shape[dim]) // (array.shape[dim] // parts)).reshape((-1,) + (1,) * (array.ndim - 1 - dim))

    first = jax.random.permutation(stream_key, parts)[block_of(target)]
    other_side = (block_of(target) + parts // 2) % parts
    return jnp.where((block_of(source) == first) | (block_of(source) == other_side), factor * array, array)


def block_levels(own_key, dims, cuts, least, high):
    level, own = 1.0, jax.random.fold_in(own_key, 6)
    for axis_at, parts in cuts:
        steps = jnp.exp(jax.random.uniform(jax.random.fold_in(own, axis_at), (parts,), jnp.float32, least / len(cuts), high / len(cuts)))
        level = level * jnp.repeat(steps, dims[axis_at] // parts).reshape([-1 if axis == axis_at else 1 for axis in range(len(dims))])
    return level


def distinct(stream_key, rows, count, top, lift):
    ranking = jax.random.permutation(jax.random.fold_in(stream_key, 1), count)
    pull = ranking
    for power in range(3):
        pull = pull * pull // count
    pull = pull * lift // count
    lots = jax.random.randint(jax.random.fold_in(stream_key, 2), (rows, count), 0, 4096) + pull
    sure = jax.random.permutation(jax.random.fold_in(stream_key, 3), rows)[jnp.arange(count) % rows]
    lots = jnp.where(jnp.arange(rows)[:, None] == sure[None, :], 1 << 14, lots)
    score = lots * count + jnp.arange(count)
    return lax.top_k(score.astype(jnp.int32), top)[1].astype(jnp.int32)


def profile(amount, total, reach, skew):
    loads = [(1 << 20) // math.isqrt(standing ** skew) + 1 for standing in range(2, amount + 1)]
    surplus, counts = total - reach - (amount - 1), [1] * (amount - 1)
    while surplus > 0:
        candidates = [i for i in range(amount - 1) if counts[i] < reach]
        whole, left = sum([loads[i] for i in candidates]), surplus
        for i in candidates:
            addition = min(reach - counts[i], max(1, left * loads[i] // whole), surplus)
            counts[i] = counts[i] + addition
            surplus = surplus - addition
    return np.array([reach] + counts)


def uneven_parts(own_key, count, total, limit, slope):
    if count == 2:
        one = jax.random.randint(own_key, (), max(1, total - limit), min(limit, total - 1) + 1)
        return jnp.stack([one, total - one])
    sizes = jnp.asarray(profile(count, total, limit, slope), jnp.int32)
    pairs = (count - 1) // 2
    giver, receiver = sizes[1:1 + 2 * pairs:2], sizes[2:2 + 2 * pairs:2]
    margin = jnp.minimum(giver - 1, limit - receiver)
    passed = jax.random.randint(jax.random.fold_in(own_key, 1), (pairs,), 0, 1 << 20) % (margin + 1)
    sizes = sizes.at[1:1 + 2 * pairs:2].set(giver - passed).at[2:2 + 2 * pairs:2].set(receiver + passed)
    return sizes[jax.random.permutation(jax.random.fold_in(own_key, 2), count)]


def centred(stream_key, shape, spread, most, shards=(), held_as=jnp.bfloat16):
    level = block_levels(stream_key, shape, shards, -0.22, 0.18) if shards else 1.0
    entries = jax.random.normal(stream_key, shape, jnp.float32) * spread * level
    return jnp.minimum(jnp.maximum(entries, -most), most).astype(held_as)


def gaussian_with(key, extent, scale, most, pieces, heavy, kind=jnp.bfloat16):
    array = scale * jax.random.normal(key, extent, jnp.float32)
    if pieces:
        array = array * block_levels(key, extent, pieces, -0.22, 0.18)
    return jnp.clip(with_spikes(array, jax.random.fold_in(key, 3), *heavy), -most, most).astype(kind)


def setup_inputs(seed: int = 0) -> dict:
    keys = jax.random.split(jax.random.key(seed), 16)
    return {
        "hidden_in": centred(keys[0], (SEQUENCE_TOTAL, SEQUENCE_LENGTH, MODEL_WIDTH), 1.0, 6.0, ((0, 4), (1, 2))),
        "doc_lengths": jax.vmap(lambda own: uneven_parts(own, DOCS, SEQUENCE_LENGTH, DOC_MOST, 2))(jax.random.split(keys[1], SEQUENCE_TOTAL)).reshape((SEQUENCE_TOTAL, DOCS)).astype(jnp.int32),
        "expert_ids": distinct(keys[2], SEQUENCE_TOTAL * SEQUENCE_LENGTH, EXPERTS, TOP, 4096).reshape((SEQUENCE_TOTAL, SEQUENCE_LENGTH, TOP)),
        "fill_rank": jax.vmap(lambda own: jax.random.permutation(own, TOK_DEV))(jax.random.split(keys[3], N_FSDP * N_CTX)).reshape((N_FSDP, N_CTX, TOK_DEV)).astype(jnp.int32),
        "norm_gains": jnp.clip(1.0 + 0.1 * jax.random.normal(keys[4], (2, MODEL_WIDTH), jnp.float32), 0.5, 1.5).astype(jnp.bfloat16),
        "qkv_weight": centred(keys[5], (MODEL_WIDTH, 3, MODEL_WIDTH), MODEL_WIDTH ** -0.5, 0.125, ((0, 8), (2, 4))),
        "qkv_bias": centred(keys[6], (3, MODEL_WIDTH), 0.2, 1.0, ((1, 4),)),
        "out_weight": centred(keys[7], (MODEL_WIDTH, MODEL_WIDTH), (max(MODEL_WIDTH // 256, 1)) ** -0.5, 2.0, ((0, 4), (1, 8))),
        "router_weight": centred(keys[8], (MODEL_WIDTH, EXPERTS), (4 * MODEL_WIDTH) ** -0.5, 0.0625),
        "blend_weight": centred(keys[9], (MODEL_WIDTH,), MODEL_WIDTH ** -0.5, 0.125),
        "shared_inner": centred(keys[10], (MODEL_WIDTH, 2, FS), MODEL_WIDTH ** -0.5, 0.125, ((0, 8), (2, 4))),
        "shared_outer": centred(keys[11], (FS, MODEL_WIDTH), (max(FS // 4, 1)) ** -0.5, 0.15625, ((0, 4), (1, 8))),
        "expert_inner": centred(keys[12], (EXPERTS, MODEL_WIDTH, 2, FE), MODEL_WIDTH ** -0.5, 0.125, ((0, 8), (3, 4))),
        "expert_outer": centred(keys[13], (EXPERTS, FE, MODEL_WIDTH), (max(FE * 8 // (EXPERTS * EXPERTS), 1)) ** -0.5, 0.4375, ((0, 8), (1, 4))),
        "cotangent": gaussian_with(keys[14], (SEQUENCE_TOTAL, SEQUENCE_LENGTH, MODEL_WIDTH), 1.0, 6.0, ((0, 4), (1, 2)), (0, 2, 4, 2.0)),
    }


@jax.custom_vjp
def low(v):
    return lax.optimization_barrier(v.astype(jnp.bfloat16)).astype(jnp.float32)

@jax.custom_vjp
def reduced_precision_back(v):
    return v

def low_keep(v):
    return (low(v), None)

def low_pass(kept, grad):
    return (grad,)

def back_keep(v):
    return (v, None)

def back_low(kept, grad):
    return (low(grad),)
low.defvjp(low_keep, low_pass)
reduced_precision_back.defvjp(back_keep, back_low)
rotary_base = 1000000.0
norm_epsilon = 1e-06
masked_score = -1e+30
highest_precision = lax.Precision.HIGHEST

def rotary_tables(positions):
    exponent = jnp.arange(HEAD_DIM // 2, dtype=jnp.float32) * (2.0 / HEAD_DIM)
    inverse = jnp.exp(-math.log(rotary_base) * exponent)
    angle = positions.astype(jnp.float32)[..., None] * inverse
    cosine = jnp.cos(angle)
    sine_table = jnp.sin(angle)
    return (jnp.concatenate([cosine, cosine], axis=-1), jnp.concatenate([sine_table, sine_table], axis=-1))

def rotate(values, cosine, sine_table):
    half_dim = values.shape[-1] // 2
    turned = jnp.concatenate([-values[..., half_dim:], values[..., :half_dim]], axis=-1)
    return values * cosine + turned * sine_table

def document_layout(lengths, positions):
    ends = jnp.cumsum(lengths).astype(jnp.int32)
    number = lax.optimization_barrier(jnp.sum((positions[:, None] >= ends[None, :-1]).astype(jnp.int32), axis=1)).astype(jnp.int32)
    starts = ends - lengths
    picked = jnp.arange(lengths.shape[0], dtype=jnp.int32)[None, :] == number[:, None]
    first = lax.optimization_barrier(jnp.sum(jnp.where(picked, starts[None, :], 0), axis=1)).astype(jnp.int32)
    return (number, positions - first)

def root_norm(values, gain):
    scale = lax.rsqrt(lax.optimization_barrier(jnp.mean(values * values, axis=-1, keepdims=True)) + norm_epsilon)
    return values * scale * gain

def to_shards(values):
    tail = values.shape[2:]
    grouped = values.reshape((N_FSDP, SEQS, N_CTX, HALF) + tail)
    grouped = jnp.swapaxes(grouped, 1, 2)
    return grouped.reshape((N_FSDP * N_CTX, TOK_DEV) + tail)

def from_shards(values):
    tail = values.shape[2:]
    grouped = values.reshape((N_FSDP, N_CTX, SEQS, HALF) + tail)
    grouped = jnp.swapaxes(grouped, 1, 2)
    return grouped.reshape((SEQUENCE_TOTAL, SEQUENCE_LENGTH) + tail)

def take_rows(table, index):
    return table[index]

def route_plan(route_rows, priority):
    onehot = (route_rows[:, :, None] == jnp.arange(EXPERTS, dtype=jnp.int32)[None, None, :]).astype(jnp.float32)
    membership = lax.optimization_barrier(jnp.sum(onehot, axis=1))
    earlier = (priority[None, :] < priority[:, None]).astype(jnp.float32)
    slot_counts = jnp.dot(earlier, membership, precision=highest_precision)
    slot_index = lax.optimization_barrier(jnp.sum(onehot * slot_counts[:, None, :], axis=2)).astype(jnp.int32)
    kept_pairs = slot_index < CAP
    flat_index = route_rows * CAP + slot_index
    target = jnp.where(kept_pairs, flat_index, EXPERTS * CAP).reshape(-1)
    token_ids = jnp.broadcast_to(jnp.arange(TOK_DEV, dtype=jnp.int32)[:, None], route_rows.shape).reshape(-1)
    source = jnp.zeros((EXPERTS * CAP,), jnp.int32).at[target].set(token_ids, mode='drop')
    filled = jnp.zeros((EXPERTS * CAP,), jnp.float32).at[target].set(1.0, mode='drop')
    return (kept_pairs.astype(jnp.float32), jnp.where(kept_pairs, flat_index, 0), source, filled)

def expert_apply(packed):
    expert_rows, inner, outer = packed
    pre = reduced_precision_back(jnp.einsum('rd,dgf->rgf', expert_rows, inner, precision=highest_precision))
    hidden = low(jax.nn.silu(pre[:, 0]) * pre[:, 1])
    return reduced_precision_back(jnp.dot(hidden, outer, precision=highest_precision))

def reference(hidden_in, doc_lengths, expert_ids, fill_rank, norm_gains, qkv_weight, qkv_bias, out_weight, router_weight, blend_weight, shared_inner, shared_outer, expert_inner, expert_outer, cotangent):
    positions = jnp.arange(SEQUENCE_LENGTH, dtype=jnp.int32)
    doc_number, doc_place = jax.vmap(document_layout, in_axes=(0, None))(doc_lengths, positions)
    cosine, sine_table = rotary_tables(doc_place)
    cosine = cosine[:, :, None, :]
    sine_table = sine_table[:, :, None, :]
    pair_onehot = (expert_ids[..., None] == jnp.arange(EXPERTS, dtype=jnp.int32)).astype(jnp.float32)
    keep_shard, pair_shard, source, filled = jax.vmap(route_plan)(to_shards(expert_ids), fill_rank.reshape(N_FSDP * N_CTX, TOK_DEV))
    score_scale = 1.0 / math.sqrt(HEAD_DIM)

    def attend(packed):
        queries, keys_all, values_all, numbers = packed
        scores = reduced_precision_back(jnp.einsum('qhd,khd->hqk', queries, keys_all, precision=highest_precision) * score_scale)
        distance = positions[:, None] - positions[None, :]
        allowed = (distance >= 0) & (distance < WINDOW) & (numbers[:, None] == numbers[None, :])
        scores = jnp.where(allowed[None], scores, masked_score)
        probabilities = jax.nn.softmax(scores, axis=-1)
        mixed_result = jnp.einsum('hqk,khd->qhd', low(probabilities), values_all, precision=highest_precision)
        return low(reduced_precision_back(mixed_result))

    def forward(hidden, gains, query_key_value_weight, query_key_value_bias, output_weight_matrix, router_weight_matrix, mixing_weight, inner_weight_matrix, outer_weight_matrix, expert_in, expert_out):
        first_normalized = low(root_norm(hidden, gains[0]))
        linear_projection = reduced_precision_back(jnp.einsum('xqp,phb->xqhb', first_normalized, query_key_value_weight, precision=highest_precision) + query_key_value_bias)
        heads = linear_projection.reshape(SEQUENCE_TOTAL, SEQUENCE_LENGTH, 3, HEADS, HEAD_DIM)
        queries = low(rotate(heads[:, :, 0], cosine, sine_table))
        keys_all = low(rotate(heads[:, :, 1], cosine, sine_table))
        values_all = low(heads[:, :, 2])
        mixed_result = lax.map(jax.checkpoint(attend), (queries, keys_all, values_all, doc_number))
        attention_output = reduced_precision_back(jnp.einsum('hqw,wg->hqg', mixed_result.reshape(SEQUENCE_TOTAL, SEQUENCE_LENGTH, MODEL_WIDTH), output_weight_matrix, precision=highest_precision))
        after_attn = hidden + attention_output
        second_normalized = low(root_norm(after_attn, gains[1]))
        router_logits = reduced_precision_back(jnp.einsum('nxi,iw->nxw', second_normalized, router_weight_matrix, precision=highest_precision))
        router_probs = jax.nn.softmax(router_logits, axis=-1)
        gate_values = lax.optimization_barrier(jnp.sum(pair_onehot * router_probs[:, :, None, :], axis=-1))
        mixing_logit = reduced_precision_back(jnp.einsum('mbh,h->mb', second_normalized, mixing_weight, precision=highest_precision))
        blend = jax.nn.sigmoid(mixing_logit)
        common_expert_preactivation = reduced_precision_back(jnp.einsum('xtz,zpj->xtpj', second_normalized, inner_weight_matrix, precision=highest_precision))
        common_expert_hidden = low(jax.nn.silu(common_expert_preactivation[..., 0, :]) * common_expert_preactivation[..., 1, :])
        common_expert_output = reduced_precision_back(jnp.einsum('bwr,rv->bwv', common_expert_hidden, outer_weight_matrix, precision=highest_precision))
        slots = jax.vmap(take_rows)(to_shards(second_normalized), source) * filled[..., None]
        expert_rows = jnp.swapaxes(slots.reshape(N_FSDP * N_CTX, EXPERTS, CAP, MODEL_WIDTH), 0, 1).reshape(EXPERTS, N_FSDP * N_CTX * CAP, MODEL_WIDTH)
        results = lax.map(jax.checkpoint(expert_apply), (expert_rows, expert_in, expert_out))
        results = jnp.swapaxes(results.reshape(EXPERTS, N_FSDP * N_CTX, CAP, MODEL_WIDTH), 0, 1).reshape(N_FSDP * N_CTX, EXPERTS * CAP, MODEL_WIDTH)
        picked = jax.vmap(take_rows)(results, pair_shard)
        pair_weights = keep_shard * to_shards(gate_values)
        expert_mix = from_shards(lax.optimization_barrier(jnp.sum(picked * pair_weights[..., None], axis=2)))
        return after_attn + blend[..., None] * common_expert_output + expert_mix
    primals = (hidden_in.astype(jnp.float32), norm_gains.astype(jnp.float32), qkv_weight.astype(jnp.float32), qkv_bias.astype(jnp.float32), out_weight.astype(jnp.float32), router_weight.astype(jnp.float32), blend_weight.astype(jnp.float32), shared_inner.astype(jnp.float32), shared_outer.astype(jnp.float32), expert_inner.astype(jnp.float32), expert_outer.astype(jnp.float32))
    result, pullback = jax.vjp(forward, *primals)
    grads = pullback(cotangent.astype(jnp.float32))
    return (result.astype(jnp.bfloat16), grads[0].astype(jnp.bfloat16), grads[1], grads[2], grads[3], grads[4], grads[5], grads[6], grads[7], grads[8], grads[9], grads[10])
```

```python
import math

import jax
import jax.numpy as jnp
from jax import lax
from jax.sharding import PartitionSpec as P

HEAD_DIM = 128
TOP = 4
WINDOW = 1024


rotary_base = 1000000.0
norm_epsilon = 1e-06
masked_score = -1e30


def from_behind(block, axis, distance):
    devices = range(lax.axis_size(axis))
    route = [(i - distance, i) for i in devices if i - distance in devices]
    return lax.ppermute(block, axis, route)


def rotary_tables(positions):
    exponent = jnp.arange(HEAD_DIM // 2, dtype=jnp.float32) * (2.0 / HEAD_DIM)
    inverse = jnp.exp(-math.log(rotary_base) * exponent)
    angle = positions.astype(jnp.float32)[..., None] * inverse
    cosine = jnp.cos(angle)
    sine_table = jnp.sin(angle)
    return (
        jnp.concatenate([cosine, cosine], axis=-1),
        jnp.concatenate([sine_table, sine_table], axis=-1),
    )


def rotate(values, cosine, sine_table):
    half_dim = values.shape[-1] // 2
    turned = jnp.concatenate([-values[..., half_dim:], values[..., :half_dim]], axis=-1)
    return values * cosine + turned * sine_table


def rotate_back(grads, cosine, sine_table):
    half_dim = grads.shape[-1] // 2
    scaled = grads * sine_table
    turned = jnp.concatenate([scaled[..., half_dim:], -scaled[..., :half_dim]], axis=-1)
    return grads * cosine + turned


def document_layout(lengths, positions):
    ends = jnp.cumsum(lengths)
    number = jnp.sum((positions[:, None] >= ends[None, :-1]).astype(jnp.int32), axis=1)
    starts = ends - lengths
    picked = jnp.arange(lengths.shape[0], dtype=jnp.int32)[None, :] == number[:, None]
    first = jnp.sum(jnp.where(picked, starts[None, :], 0), axis=1)
    return (number, positions - first)


def root_norm(values, gain):
    scale = lax.rsqrt(jnp.mean(values * values, axis=-1, keepdims=True) + norm_epsilon)
    return values * scale * gain


def silu_parts(gate_pre):
    sigma = jax.nn.sigmoid(gate_pre)
    return (gate_pre * sigma, sigma * (1.0 + gate_pre * (1.0 - sigma)))


def attend_forward(queries, keys_all, values_all, allowed, score_scale):
    scores = (
        jnp.einsum("qhd,khd->hqk", queries, keys_all, preferred_element_type=jnp.float32)
        * score_scale
    )
    scores = jnp.where(allowed[None], scores, masked_score)
    row_max = jnp.max(scores, axis=-1, keepdims=True)
    row_total = jnp.sum(jnp.exp(scores - row_max), axis=-1, keepdims=True)
    log_total = row_max + jnp.log(row_total)
    weights_low = jnp.exp(scores - log_total).astype(jnp.bfloat16)
    mixed_result = jnp.einsum(
        "hqk,khd->qhd", weights_low, values_all, preferred_element_type=jnp.float32
    )
    return (mixed_result.astype(jnp.bfloat16), log_total)


def attend_backward(queries, keys_all, values_all, allowed, log_total, grad_mixed, score_scale):
    scores = (
        jnp.einsum("qhd,khd->hqk", queries, keys_all, preferred_element_type=jnp.float32)
        * score_scale
    )
    scores = jnp.where(allowed[None], scores, masked_score)
    soft = jnp.exp(scores - log_total)
    grad_soft = jnp.einsum(
        "qhd,khd->hqk", grad_mixed, values_all, preferred_element_type=jnp.float32
    )
    centre = jnp.sum(soft * grad_soft, axis=-1, keepdims=True)
    grad_scores = (soft * (grad_soft - centre)).astype(jnp.bfloat16)
    grad_queries = (
        jnp.einsum("hqk,khd->qhd", grad_scores, keys_all, preferred_element_type=jnp.float32)
        * score_scale
    )
    grad_keys = (
        jnp.einsum("hqk,qhd->khd", grad_scores, queries, preferred_element_type=jnp.float32)
        * score_scale
    )
    grad_values = jnp.einsum(
        "hqk,qhd->khd", soft.astype(jnp.bfloat16), grad_mixed, preferred_element_type=jnp.float32
    )
    return (grad_queries, grad_keys, grad_values)


def general_plan(
    hidden_in,
    doc_lengths,
    expert_ids,
    fill_rank,
    norm_gains,
    qkv_weight,
    qkv_bias,
    out_weight,
    router_weight,
    blend_weight,
    shared_inner,
    shared_outer,
    expert_inner,
    expert_outer,
    cotangent,
):
    seq_count, half_len, width = hidden_in.shape
    tokens = seq_count * half_len
    local_width = qkv_weight.shape[2]
    local_heads = local_width // HEAD_DIM
    experts = router_weight.shape[1]
    expert_local = expert_inner.shape[0]
    groups = experts // expert_local
    capacity = tokens * TOP // experts
    score_scale = 1.0 / math.sqrt(HEAD_DIM)
    gains = norm_gains.astype(jnp.float32)
    qkv_full, out_full, inner_full, outer_full = (
        lax.all_gather(qkv_weight, ("fsdp", "ctx"), axis=0, tiled=True),
        lax.all_gather(out_weight, ("fsdp", "ctx"), axis=1, tiled=True),
        lax.all_gather(shared_inner, ("fsdp", "ctx"), axis=0, tiled=True),
        lax.all_gather(shared_outer, ("fsdp", "ctx"), axis=1, tiled=True),
    )
    positions = lax.axis_index("ctx") * half_len + jnp.arange(half_len, dtype=jnp.int32)
    earlier_pos = positions - half_len
    own_number, own_place = jax.vmap(document_layout, in_axes=(0, None))(doc_lengths, positions)
    prior_number = jax.vmap(document_layout, in_axes=(0, None))(doc_lengths, earlier_pos)[0]
    cosine, sine_table = rotary_tables(own_place)
    cosine = cosine[:, :, None, :]
    sine_table = sine_table[:, :, None, :]
    key_positions = jnp.concatenate([earlier_pos, positions])
    distance = positions[:, None] - key_positions[None, :]
    base_allowed = (distance >= 0) & (distance < WINDOW) & (key_positions[None, :] >= 0)
    key_numbers = jnp.concatenate([prior_number, own_number], axis=1)
    allowed = base_allowed[None] & (own_number[:, :, None] == key_numbers[:, None, :])
    residual = hidden_in.reshape(tokens, width).astype(jnp.float32)
    first_normalized = root_norm(residual, gains[0]).astype(jnp.bfloat16)
    linear_projection = (
        jnp.einsum("td,dcm->tcm", first_normalized, qkv_full, preferred_element_type=jnp.float32)
        + qkv_bias.astype(jnp.float32)[None]
    )
    heads = linear_projection.reshape(seq_count, half_len, 3, local_heads, HEAD_DIM)
    queries = rotate(heads[:, :, 0], cosine, sine_table).astype(jnp.bfloat16)
    keys_own = rotate(heads[:, :, 1], cosine, sine_table).astype(jnp.bfloat16)
    values_own = heads[:, :, 2].astype(jnp.bfloat16)
    keys_prior, values_prior = from_behind((keys_own, values_own), "ctx", 1)
    keys_all = jnp.concatenate([keys_prior, keys_own], axis=1)
    values_all = jnp.concatenate([values_prior, values_own], axis=1)
    sequence = 0
    mixed_one, log_one = attend_forward(
        queries[sequence], keys_all[sequence], values_all[sequence], allowed[sequence], score_scale
    )
    mixed_parts = [mixed_one]
    log_parts = [log_one]
    mixed_result = jnp.stack(mixed_parts).reshape(tokens, local_width)
    attn_part = jnp.dot(mixed_result, out_full, preferred_element_type=jnp.float32)
    after_attn = residual + lax.psum(attn_part, "tp")
    second_normalized = root_norm(after_attn, gains[1]).astype(jnp.bfloat16)
    router_logits = jnp.dot(second_normalized, router_weight, preferred_element_type=jnp.float32)
    router_probs = jax.nn.softmax(router_logits, axis=-1)
    route_rows = expert_ids.reshape(tokens, TOP)
    onehot = (route_rows[:, :, None] == jnp.arange(experts, dtype=jnp.int32)[None, None, :]).astype(
        jnp.float32
    )
    gate_values = jnp.sum(onehot * router_probs[:, None, :], axis=-1)
    membership = jnp.sum(onehot, axis=1).astype(jnp.bfloat16)
    priority = fill_rank.reshape(tokens)
    earlier = (priority[None, :] < priority[:, None]).astype(jnp.bfloat16)
    slot_counts = jnp.dot(earlier, membership, preferred_element_type=jnp.float32)
    slot_index = jnp.sum(onehot * slot_counts[:, None, :], axis=-1).astype(jnp.int32)
    kept_pairs = slot_index < capacity
    keep_weight = kept_pairs.astype(jnp.float32)
    flat_index = route_rows * capacity + slot_index
    target = jnp.where(kept_pairs, flat_index, experts * capacity).reshape(-1)
    pair_index = jnp.where(kept_pairs, flat_index, 0)
    token_ids = jnp.broadcast_to(
        jnp.arange(tokens, dtype=jnp.int32)[:, None], (tokens, TOP)
    ).reshape(-1)
    source = jnp.zeros((experts * capacity,), jnp.int32).at[target].set(token_ids, mode="drop")
    filled = jnp.zeros((experts * capacity,), jnp.bool_).at[target].set(True, mode="drop")
    slot_gate = (
        jnp.zeros((experts * capacity,), jnp.float32)
        .at[target]
        .set(gate_values.reshape(-1), mode="drop")
    )
    dispatch = jnp.where(filled[:, None], second_normalized[source], jnp.zeros((), jnp.bfloat16))
    expert_rows = lax.all_to_all(
        dispatch.reshape(groups, expert_local, capacity, width),
        ("fsdp", "ctx"),
        split_axis=0,
        concat_axis=2,
        tiled=True,
    )[0]
    expert_pre = jnp.einsum(
        "erd,edgf->ergf", expert_rows, expert_inner, preferred_element_type=jnp.float32
    )
    expert_act, expert_slope = silu_parts(expert_pre[:, :, 0])
    expert_hidden = (expert_act * expert_pre[:, :, 1]).astype(jnp.bfloat16)
    expert_result = jnp.einsum(
        "erf,efd->erd", expert_hidden, expert_outer, preferred_element_type=jnp.float32
    )
    returned = (
        lax.all_to_all(
            expert_result[None].astype(jnp.bfloat16),
            ("fsdp", "ctx"),
            split_axis=2,
            concat_axis=0,
            tiled=True,
        )
        .astype(jnp.float32)
        .reshape(experts * capacity, width)
    )
    common_expert_preactivation = jnp.einsum(
        "td,dgf->tgf", second_normalized, inner_full, preferred_element_type=jnp.float32
    )
    shared_act, shared_slope = silu_parts(common_expert_preactivation[:, 0])
    common_expert_hidden = (shared_act * common_expert_preactivation[:, 1]).astype(jnp.bfloat16)
    shared_part = jnp.dot(common_expert_hidden, outer_full, preferred_element_type=jnp.float32)
    blend = jax.nn.sigmoid(
        jnp.dot(second_normalized, blend_weight, preferred_element_type=jnp.float32)
    )
    expert_part = jnp.zeros((tokens, width), jnp.float32)
    for route_slot in range(TOP):
        expert_part = (
            expert_part
            + (keep_weight[:, route_slot] * gate_values[:, route_slot])[:, None]
            * returned[pair_index[:, route_slot]]
        )
    branch = lax.psum(
        (blend[:, None] * shared_part + expert_part).astype(jnp.bfloat16), "tp"
    ).astype(jnp.float32)
    layer_out = (after_attn + branch).astype(jnp.bfloat16).reshape(seq_count, half_len, width)
    grad_y = cotangent.reshape(tokens, width).astype(jnp.float32)
    shared_dot = jnp.sum(grad_y * shared_part, axis=-1)
    gate_dots = []
    for route_slot in range(TOP):
        gate_dots.append(jnp.sum(grad_y * returned[pair_index[:, route_slot]], axis=-1))
    gate_dot = jnp.stack(gate_dots, axis=1)
    grad_shared = (blend[:, None] * grad_y).astype(jnp.bfloat16)
    grad_shared_hidden = jnp.einsum(
        "td,fd->tf", grad_shared, outer_full, preferred_element_type=jnp.float32
    )
    grad_shared_pre = jnp.stack(
        [
            grad_shared_hidden * common_expert_preactivation[:, 1] * shared_slope,
            grad_shared_hidden * shared_act,
        ],
        axis=1,
    ).astype(jnp.bfloat16)
    inner_grad_full = jnp.einsum(
        "td,tgf->dgf", second_normalized, grad_shared_pre, preferred_element_type=jnp.float32
    )
    outer_grad_full = jnp.einsum(
        "tf,td->fd", common_expert_hidden, grad_shared, preferred_element_type=jnp.float32
    )
    grad_normed_part = jnp.einsum(
        "tgf,dgf->td", grad_shared_pre, inner_full, preferred_element_type=jnp.float32
    )
    grad_result = jnp.where(filled[:, None], slot_gate[:, None] * grad_y[source], 0.0).astype(
        jnp.bfloat16
    )
    grad_rows_in = lax.all_to_all(
        grad_result.reshape(groups, expert_local, capacity, width),
        ("fsdp", "ctx"),
        split_axis=0,
        concat_axis=2,
        tiled=True,
    )[0]
    grad_expert_hidden = jnp.einsum(
        "erd,efd->erf", grad_rows_in, expert_outer, preferred_element_type=jnp.float32
    )
    grad_expert_pre = jnp.stack(
        [grad_expert_hidden * expert_pre[:, :, 1] * expert_slope, grad_expert_hidden * expert_act],
        axis=2,
    ).astype(jnp.bfloat16)
    outer_expert = jnp.einsum(
        "erf,erd->efd", expert_hidden, grad_rows_in, preferred_element_type=jnp.float32
    )
    inner_expert = jnp.einsum(
        "erd,ergf->edgf", expert_rows, grad_expert_pre, preferred_element_type=jnp.float32
    )
    grad_rows_out = jnp.einsum(
        "ergf,edgf->erd", grad_expert_pre, expert_inner, preferred_element_type=jnp.float32
    )
    returned_back = (
        lax.all_to_all(
            grad_rows_out[None].astype(jnp.bfloat16),
            ("fsdp", "ctx"),
            split_axis=2,
            concat_axis=0,
            tiled=True,
        )
        .astype(jnp.float32)
        .reshape(experts * capacity, width)
    )
    for route_slot in range(TOP):
        grad_normed_part = (
            grad_normed_part
            + keep_weight[:, route_slot][:, None] * returned_back[pair_index[:, route_slot]]
        )
    grad_normed_sum, shared_total, gate_total = lax.psum(
        (grad_normed_part, shared_dot, gate_dot), "tp"
    )
    grad_blend = (blend * (1.0 - blend) * shared_total).astype(jnp.bfloat16)
    grad_gate = keep_weight * gate_total
    grad_probs = jnp.sum(onehot * grad_gate[:, :, None], axis=1)
    grad_logits = (
        router_probs * (grad_probs - jnp.sum(router_probs * grad_probs, axis=-1, keepdims=True))
    ).astype(jnp.bfloat16)
    router_grad_part = jnp.einsum(
        "td,te->de", second_normalized, grad_logits, preferred_element_type=jnp.float32
    )
    blend_grad_part = jnp.einsum(
        "td,t->d", second_normalized, grad_blend, preferred_element_type=jnp.float32
    )
    grad_normed_two = (
        grad_normed_sum
        + jnp.einsum("te,de->td", grad_logits, router_weight, preferred_element_type=jnp.float32)
        + grad_blend.astype(jnp.float32)[:, None] * blend_weight.astype(jnp.float32)[None, :]
    )
    after_norm_grad, gain_two_grad = jax.vjp(root_norm, after_attn, gains[1])[1](grad_normed_two)
    grad_after = grad_y + after_norm_grad
    grad_attn = grad_after.astype(jnp.bfloat16)
    projection_full = jnp.einsum(
        "tm,td->md", mixed_result, grad_attn, preferred_element_type=jnp.float32
    )
    grad_mixed = (
        jnp.einsum("td,md->tm", grad_attn, out_full, preferred_element_type=jnp.float32)
        .astype(jnp.bfloat16)
        .reshape(seq_count, half_len, local_heads, HEAD_DIM)
    )
    sequence = 0
    grad_query, grad_key, grad_value = attend_backward(
        queries[sequence],
        keys_all[sequence],
        values_all[sequence],
        allowed[sequence],
        log_parts[sequence],
        grad_mixed[sequence],
        score_scale,
    )
    query_parts = [grad_query]
    key_parts = [grad_key]
    value_parts = [grad_value]
    grad_queries = jnp.stack(query_parts)
    grad_keys = jnp.stack(key_parts)
    grad_values = jnp.stack(value_parts)
    sent_keys, sent_values = (
        from_behind(grad_keys[:, :half_len].astype(jnp.bfloat16), "ctx", -1).astype(jnp.float32),
        from_behind(grad_values[:, :half_len].astype(jnp.bfloat16), "ctx", -1).astype(jnp.float32),
    )
    grad_keys_own = grad_keys[:, half_len:] + sent_keys
    grad_values_own = grad_values[:, half_len:] + sent_values
    grad_linear = (
        jnp.stack(
            [
                rotate_back(grad_queries, cosine, sine_table),
                rotate_back(grad_keys_own, cosine, sine_table),
                grad_values_own,
            ],
            axis=2,
        )
        .astype(jnp.bfloat16)
        .reshape(tokens, 3, local_width)
    )
    bias_part = jnp.sum(grad_linear.astype(jnp.float32), axis=0)
    qkv_grad_full = jnp.einsum(
        "td,tcm->dcm", first_normalized, grad_linear, preferred_element_type=jnp.float32
    )
    grad_normed_one = lax.psum(
        jnp.einsum("tcm,dcm->td", grad_linear, qkv_full, preferred_element_type=jnp.float32).astype(
            jnp.bfloat16
        ),
        "tp",
    ).astype(jnp.float32)
    residual_norm_grad, gain_one_grad = jax.vjp(root_norm, residual, gains[0])[1](grad_normed_one)
    input_grad = (
        (grad_after + residual_norm_grad).astype(jnp.bfloat16).reshape(seq_count, half_len, width)
    )
    qkv_grad, projection_grad, inner_shared, outer_shared = (
        lax.psum_scatter(
            qkv_grad_full.astype(jnp.bfloat16), ("fsdp", "ctx"), scatter_dimension=0, tiled=True
        ).astype(jnp.float32),
        lax.psum_scatter(
            projection_full.astype(jnp.bfloat16), ("fsdp", "ctx"), scatter_dimension=1, tiled=True
        ).astype(jnp.float32),
        lax.psum_scatter(
            inner_grad_full.astype(jnp.bfloat16), ("fsdp", "ctx"), scatter_dimension=0, tiled=True
        ).astype(jnp.float32),
        lax.psum_scatter(
            outer_grad_full.astype(jnp.bfloat16), ("fsdp", "ctx"), scatter_dimension=1, tiled=True
        ).astype(jnp.float32),
    )
    gains_grad, bias_grad, router_grad, blend_grad = (
        lax.psum(
            jnp.stack([gain_one_grad, gain_two_grad]).astype(jnp.bfloat16), ("fsdp", "ctx")
        ).astype(jnp.float32),
        lax.psum(bias_part.astype(jnp.bfloat16), ("fsdp", "ctx")).astype(jnp.float32),
        lax.psum(router_grad_part.astype(jnp.bfloat16), ("fsdp", "ctx")).astype(jnp.float32),
        lax.psum(blend_grad_part.astype(jnp.bfloat16), ("fsdp", "ctx")).astype(jnp.float32),
    )
    return (
        layer_out,
        input_grad,
        gains_grad,
        qkv_grad,
        bias_grad,
        projection_grad,
        router_grad,
        blend_grad,
        inner_shared,
        outer_shared,
        inner_expert,
        outer_expert,
    )


def after(values, *earlier):
    return lax.optimization_barrier((values, earlier))[0]


def swap_x(values):
    return lax.ppermute(values, "fsdp", [(f, f ^ 2) for f in range(4)])


def swap_core(values):
    return lax.ppermute(values, "fsdp", [(f, f ^ 1) for f in range(4)])


def swap_y(values):
    return lax.ppermute(values, "ctx", [(0, 1), (1, 0)])


def own_number():
    return lax.axis_index("fsdp") * 2 + lax.axis_index("ctx")


def exchange_order(parts):
    number = own_number()
    for bit in (4, 2, 1):
        taken = (number & bit) != 0
        parts = [jnp.where(taken, parts[i ^ bit], parts[i]) for i in range(8)]
    return parts


def spread_chips(block):
    half = block.shape[0] // 2
    from_x = swap_x(block)
    from_y = swap_y(block)
    low_part = swap_x(from_y[:half])
    high_part = swap_y(from_x[half:])
    return [block, from_y, from_x, jnp.concatenate([low_part, high_part])]


def gather_eight(block):
    own, from_y, from_x, from_both = spread_chips(block)
    return [
        own,
        from_y,
        swap_core(own),
        swap_core(from_y),
        from_x,
        from_both,
        swap_core(from_x),
        swap_core(from_both),
    ]


def add_low(one, other):
    return (one.astype(jnp.float32) + other.astype(jnp.float32)).astype(jnp.bfloat16)


def reduce_chips(own, for_y, for_x, for_both):
    half = own.shape[0] // 2
    low_part = swap_x(for_both[:half])
    high_part = swap_y(for_both[half:])
    for_y = jnp.concatenate([add_low(for_y[:half], low_part), for_y[half:]])
    for_x = jnp.concatenate([for_x[:half], add_low(for_x[half:], high_part)])
    return (
        own.astype(jnp.float32)
        + swap_x(for_x).astype(jnp.float32)
        + swap_y(for_y).astype(jnp.float32)
    )


def reduce_eight(parts):
    return reduce_chips(
        add_low(parts[0], swap_core(parts[2])),
        add_low(parts[1], swap_core(parts[3])),
        add_low(parts[4], swap_core(parts[6])),
        add_low(parts[5], swap_core(parts[7])),
    )


def trade_eight(parts):
    rows = parts[0].shape[0]
    from_y = swap_y(jnp.concatenate([parts[1], parts[3]]))
    from_x = swap_x(jnp.concatenate([parts[4], parts[6]]))
    both = lax.ppermute(
        jnp.concatenate([parts[5], parts[7]]),
        ("fsdp", "ctx"),
        [(d, d ^ 5) for d in range(8)],
    )
    sibling = swap_core(
        jnp.concatenate([parts[2], from_y[rows:], from_x[rows:], both[rows:]])
    )
    return [
        parts[0],
        from_y[:rows],
        sibling[:rows],
        sibling[rows : 2 * rows],
        from_x[:rows],
        both[:rows],
        sibling[2 * rows : 3 * rows],
        sibling[3 * rows :],
    ]


def pick(blocks, index):
    return lax.dynamic_index_in_dim(blocks, index, axis=0, keepdims=False)


def line_gather(block):
    count = lax.axis_size("tp")
    me = lax.axis_index("tp")
    right, left = block, block
    result = jnp.broadcast_to(block[None], (count,) + block.shape)
    for step in range(1, count):
        right = lax.ppermute(right, "tp", [(i, i + 1) for i in range(step - 1, count - 1)])
        left = lax.ppermute(left, "tp", [(i, i - 1) for i in range(1, count - step + 1)])
        place = jnp.arange(count, dtype=jnp.int32).reshape((count,) + (1,) * block.ndim)
        result = jnp.where(
            place == me - step, right[None], jnp.where(place == me + step, left[None], result)
        )
    return result


def line_reduce(blocks):
    count = blocks.shape[0]
    me = lax.axis_index("tp")
    right, left = None, None
    for step in range(1, count):
        to_right = pick(blocks, jnp.minimum(count - step + me, count - 1))
        to_left = pick(blocks, jnp.maximum(step + me - count, 0))
        if step > 1:
            to_right, to_left = add_low(to_right, right), add_low(to_left, left)
        right = lax.ppermute(to_right, "tp", [(i, i + 1) for i in range(min(step, count - 1))])
        left = lax.ppermute(
            to_left, "tp", [(i, i - 1) for i in range(max(count - step, 1), count)]
        )
    return (
        pick(blocks, me).astype(jnp.float32)
        + right.astype(jnp.float32)
        + left.astype(jnp.float32)
    )


def columns_of(values, count):
    wide = values.shape[1] // count
    return [values[:, i * wide : (i + 1) * wide] for i in range(count)]


def mixture_chunk(rows, grads, kept, inner, outer, mine, sizes):
    hid_e, hid, pad, experts = sizes
    pre = lax.dot_general(
        rows, inner, (((1,), (1,)), ((), ())), preferred_element_type=jnp.float32
    )
    upstream = lax.dot_general(
        grads, outer, (((1,), (1,)), ((), ())), preferred_element_type=jnp.float32
    )
    gate_pre = pre[:, :hid]
    up_pre = pre[:, pad:]
    probs = jax.nn.softmax(pre[:, hid : hid + experts], axis=-1)
    own_prob = jnp.sum(probs * mine, axis=-1, keepdims=True)
    blend = jax.nn.sigmoid(pre[:, hid + experts : hid + experts + 1])
    gate = kept * own_prob
    of_expert = jnp.arange(hid)[None, :] < hid_e
    weight = jnp.where(of_expert, gate, blend)
    act, slope = silu_parts(gate_pre)
    hidden = (act * up_pre).astype(jnp.bfloat16).astype(jnp.float32)
    product = hidden * upstream
    gate_dot = kept * jnp.sum(jnp.where(of_expert, product, 0.0), axis=-1, keepdims=True)
    blend_dot = jnp.sum(jnp.where(of_expert, 0.0, product), axis=-1, keepdims=True)
    grad_logits = probs * gate_dot * (mine - own_prob)
    grad_blend = blend * (1.0 - blend) * blend_dot
    scaled = weight * upstream
    grad_pre = jnp.concatenate(
        [
            scaled * up_pre * slope,
            grad_logits,
            grad_blend,
            jnp.zeros((rows.shape[0], pad - hid - experts - 1), jnp.float32),
            scaled * act,
        ],
        axis=1,
    ).astype(jnp.bfloat16)
    weighted = (weight * hidden).astype(jnp.bfloat16)
    back = jnp.dot(grad_pre, inner, preferred_element_type=jnp.float32).astype(jnp.bfloat16)
    return (grad_pre, weighted, back)


def eight_plan(
    hidden_in,
    doc_lengths,
    expert_ids,
    fill_rank,
    norm_gains,
    qkv_weight,
    qkv_bias,
    out_weight,
    router_weight,
    blend_weight,
    shared_inner,
    shared_outer,
    expert_inner,
    expert_outer,
    cotangent,
):
    _, tokens, width = hidden_in.shape
    local_width = qkv_weight.shape[2]
    local_heads = local_width // HEAD_DIM
    experts = router_weight.shape[1]
    capacity = tokens * TOP // experts
    score_scale = 1.0 / math.sqrt(HEAD_DIM)
    gains = norm_gains.astype(jnp.float32)
    me_tp = lax.axis_index("tp")
    tp = lax.axis_size("tp")
    share = tokens // tp
    number = own_number()

    def own_rows(values):
        return lax.dynamic_slice_in_dim(values, me_tp * share, share, axis=0)

    qkv_parts = gather_eight(qkv_weight)
    qkv_rel = jnp.concatenate(qkv_parts, axis=0)

    route_rows = expert_ids.reshape(tokens, TOP)
    named = jnp.sum(
        (route_rows[:, :, None] == jnp.arange(experts, dtype=jnp.int32)[None, None, :]).astype(
            jnp.float32
        ),
        axis=1,
    )
    priority = fill_rank.reshape(tokens)
    earlier = (priority[None, :] < priority[:, None]).astype(jnp.bfloat16)
    slot_counts = jnp.dot(
        earlier, named.astype(jnp.bfloat16), preferred_element_type=jnp.float32
    )
    kept_all = named * (slot_counts < capacity).astype(jnp.float32)
    kept_blocks = lax.all_to_all(
        kept_all.T.reshape(experts, 1, tokens),
        ("fsdp", "ctx"),
        split_axis=0,
        concat_axis=0,
        tiled=True,
    )
    kept_rel = exchange_order([kept_blocks[i].reshape(tokens, 1) for i in range(8)])

    half_len = tokens
    positions = lax.axis_index("ctx") * half_len + jnp.arange(half_len, dtype=jnp.int32)
    earlier_pos = positions - half_len
    own_number_doc, own_place = document_layout(doc_lengths[0], positions)
    prior_number = document_layout(doc_lengths[0], earlier_pos)[0]
    cosine, sine_table = rotary_tables(own_place)
    cosine = cosine[:, None, :]
    sine_table = sine_table[:, None, :]
    key_positions = jnp.concatenate([earlier_pos, positions])
    distance = positions[:, None] - key_positions[None, :]
    key_numbers = jnp.concatenate([prior_number, own_number_doc])
    allowed = (
        (distance >= 0)
        & (distance < WINDOW)
        & (key_positions[None, :] >= 0)
        & (own_number_doc[:, None] == key_numbers[None, :])
    )
    residual = hidden_in.reshape(tokens, width).astype(jnp.float32)
    first_normalized = root_norm(residual, gains[0]).astype(jnp.bfloat16)
    first_rel = jnp.concatenate(exchange_order(columns_of(first_normalized, 8)), axis=1)
    linear_projection = (
        jnp.einsum("td,dcm->tcm", first_rel, qkv_rel, preferred_element_type=jnp.float32)
        + qkv_bias.astype(jnp.float32)[None]
    )
    heads = linear_projection.reshape(tokens, 3, local_heads, HEAD_DIM)
    queries = rotate(heads[:, 0], cosine, sine_table).astype(jnp.bfloat16)
    keys_own = rotate(heads[:, 1], cosine, sine_table).astype(jnp.bfloat16)
    values_own = heads[:, 2].astype(jnp.bfloat16)
    keys_prior, values_prior = from_behind((keys_own, values_own), "ctx", 1)
    keys_all = jnp.concatenate([keys_prior, keys_own], axis=0)
    values_all = jnp.concatenate([values_prior, values_own], axis=0)

    shared_t = jnp.transpose(after(shared_inner, qkv_parts[5]), (1, 2, 0))
    hid_s = shared_t.shape[1] // 8
    pieces = [
        jnp.concatenate(
            [
                shared_t[0, d * hid_s : (d + 1) * hid_s],
                shared_t[1, d * hid_s : (d + 1) * hid_s],
                shared_outer[d * hid_s : (d + 1) * hid_s],
            ]
        )
        for d in range(8)
    ]
    shared_rows = jnp.concatenate(
        exchange_order(trade_eight(exchange_order(pieces))), axis=1
    )
    out_own = jnp.concatenate(
        exchange_order(gather_eight(after(out_weight, qkv_parts[5]))), axis=1
    )
    half_rows = local_width // 2
    core = lax.axis_index("fsdp") % 2
    out_half = line_gather(
        lax.dynamic_slice_in_dim(out_own, core * half_rows, half_rows, axis=0)
    )
    out_other = swap_core(out_half)
    out_full = jnp.stack(
        [
            jnp.where(core == 0, out_half, out_other),
            jnp.where(core == 0, out_other, out_half),
        ],
        axis=1,
    ).reshape(tp * local_width, width)

    mixed_result, log_total = attend_forward(queries, keys_all, values_all, allowed, score_scale)
    mixed_result = mixed_result.reshape(tokens, local_width)

    grad_rows = cotangent.reshape(tokens, width)
    grad_parts = gather_eight(after(grad_rows, keys_prior, values_prior, shared_rows))

    mixed_all = line_gather(mixed_result)
    attended = jnp.concatenate([mixed_all[i] for i in range(tp)], axis=1)
    after_attn = residual + jnp.dot(attended, out_full, preferred_element_type=jnp.float32)
    second_normalized = root_norm(after_attn, gains[1]).astype(jnp.bfloat16)

    hid_e = expert_inner.shape[3]
    hid = hid_e + hid_s
    pad = -(-(hid + experts + 1) // 128) * 128
    expert_t = jnp.transpose(expert_inner[0], (1, 2, 0))
    inner = jnp.concatenate(
        [
            expert_t[0],
            shared_rows[:hid_s],
            router_weight.T,
            blend_weight[None],
            jnp.zeros((pad - hid - experts - 1, width), jnp.bfloat16),
            expert_t[1],
            shared_rows[hid_s : 2 * hid_s],
        ]
    )
    outer = jnp.concatenate([expert_outer[0], shared_rows[2 * hid_s :]])
    mine = (jnp.arange(experts, dtype=jnp.int32) == number).astype(jnp.float32)[None]
    sizes = (hid_e, hid, pad, experts)

    row_parts = gather_eight(after(second_normalized, grad_parts[5]))
    pre_list, weighted_list, back_list = [], [], []
    for pair in (0, 1, 4, 5):
        grad_pre, weighted, back = mixture_chunk(
            jnp.concatenate([row_parts[pair], row_parts[pair + 2]]),
            jnp.concatenate([grad_parts[pair], grad_parts[pair + 2]]),
            jnp.concatenate([kept_rel[pair], kept_rel[pair + 2]]),
            inner,
            outer,
            mine,
            sizes,
        )
        pre_list.append(grad_pre)
        weighted_list.append(weighted)
        back_list.append(back)

    def to_chips(chunks):
        return reduce_chips(
            *[add_low(chunk[:tokens], swap_core(chunk[tokens:])) for chunk in chunks]
        ).astype(jnp.bfloat16)

    back_sum = to_chips(back_list)
    grad_normed_two = line_reduce(back_sum.reshape(tp, share, width))

    forward_list = [
        jnp.dot(w, outer, preferred_element_type=jnp.float32).astype(jnp.bfloat16)
        for w in weighted_list
    ]
    forward_list = after(forward_list, back_sum)
    forward_sum = to_chips(forward_list)

    grad_y = own_rows(grad_rows).astype(jnp.float32)
    after_own = own_rows(after_attn)
    after_norm_grad, gain_two_grad = jax.vjp(root_norm, after_own, gains[1])[1](grad_normed_two)
    grad_after = grad_y + after_norm_grad
    grad_attn = line_gather(grad_after.astype(jnp.bfloat16)).reshape(tokens, width)

    grad_mixed = lax.dot_general(
        grad_attn, out_own, (((1,), (1,)), ((), ())), preferred_element_type=jnp.float32
    )
    grad_mixed = grad_mixed.astype(jnp.bfloat16).reshape(tokens, local_heads, HEAD_DIM)
    grad_query, grad_key, grad_value = attend_backward(
        queries, keys_all, values_all, allowed, log_total, grad_mixed, score_scale
    )
    sent_keys, sent_values = from_behind(
        (grad_key[:half_len].astype(jnp.bfloat16), grad_value[:half_len].astype(jnp.bfloat16)),
        "ctx",
        -1,
    )
    grad_linear = (
        jnp.stack(
            [
                rotate_back(grad_query, cosine, sine_table),
                rotate_back(
                    grad_key[half_len:] + sent_keys.astype(jnp.float32), cosine, sine_table
                ),
                grad_value[half_len:] + sent_values.astype(jnp.float32),
            ],
            axis=1,
        )
        .astype(jnp.bfloat16)
        .reshape(tokens, 3, local_width)
    )
    grad_one_part = jnp.einsum(
        "tcm,dcm->td", grad_linear, qkv_rel, preferred_element_type=jnp.float32
    ).astype(jnp.bfloat16)
    grad_one_rel = line_reduce(grad_one_part.reshape(tp, share, width))
    grad_normed_one = jnp.concatenate(exchange_order(columns_of(grad_one_rel, 8)), axis=1)
    residual_norm_grad, gain_one_grad = jax.vjp(root_norm, own_rows(residual), gains[0])[1](
        grad_normed_one
    )
    input_grad = line_gather((grad_after + residual_norm_grad).astype(jnp.bfloat16)).reshape(
        1, tokens, width
    )

    layer_own = own_rows(after_attn) + line_reduce(forward_sum.reshape(tp, share, width))
    layer_out = line_gather(layer_own.astype(jnp.bfloat16)).reshape(1, tokens, width)

    qkv_full = jnp.einsum(
        "td,tcm->dcm", first_rel, grad_linear, preferred_element_type=jnp.float32
    ).astype(jnp.bfloat16)
    rows_each = width // 8
    qkv_grad = reduce_eight([qkv_full[i * rows_each : (i + 1) * rows_each] for i in range(8)])
    projection_full = lax.dot_general(
        mixed_result, grad_attn, (((0,), (0,)), ((), ())), preferred_element_type=jnp.float32
    ).astype(jnp.bfloat16)
    projection_grad = reduce_eight(exchange_order(columns_of(projection_full, 8)))

    all_rows = jnp.concatenate([row_parts[i] for p in (0, 1, 4, 5) for i in (p, p + 2)])
    all_grads = jnp.concatenate([grad_parts[i] for p in (0, 1, 4, 5) for i in (p, p + 2)])
    inner_grad = lax.dot_general(
        jnp.concatenate(pre_list),
        all_rows,
        (((0,), (0,)), ((), ())),
        preferred_element_type=jnp.float32,
    )
    outer_grad = lax.dot_general(
        jnp.concatenate(weighted_list),
        all_grads,
        (((0,), (0,)), ((), ())),
        preferred_element_type=jnp.float32,
    )
    inner_expert = jnp.transpose(
        jnp.stack([inner_grad[:hid_e], inner_grad[pad : pad + hid_e]]), (2, 0, 1)
    )[None]
    outer_expert = outer_grad[:hid_e][None]
    shared_grad = jnp.concatenate(
        [inner_grad[hid_e:hid], inner_grad[pad + hid_e :], outer_grad[hid_e:]]
    ).astype(jnp.bfloat16)
    shared_parts = exchange_order(trade_eight(exchange_order(columns_of(shared_grad, 8))))
    inner_shared = jnp.transpose(
        jnp.stack(
            [
                jnp.concatenate([p[:hid_s] for p in shared_parts]),
                jnp.concatenate([p[hid_s : 2 * hid_s] for p in shared_parts]),
            ]
        ),
        (2, 0, 1),
    ).astype(jnp.float32)
    outer_shared = jnp.concatenate([p[2 * hid_s :] for p in shared_parts]).astype(jnp.float32)

    everywhere = ("fsdp", "ctx", "tp")
    small = lax.psum(
        jnp.concatenate(
            [
                inner_grad[hid : hid + experts + 1],
                gain_one_grad[None],
                gain_two_grad[None],
            ]
        ),
        everywhere,
    )
    router_grad = small[:experts].T
    blend_grad = small[experts]
    gains_grad = small[experts + 1 :]
    bias_grad = lax.psum(jnp.sum(grad_linear.astype(jnp.float32), axis=0), ("fsdp", "ctx"))
    return (
        layer_out,
        input_grad,
        gains_grad,
        qkv_grad,
        bias_grad,
        projection_grad,
        router_grad,
        blend_grad,
        inner_shared,
        outer_shared,
        inner_expert,
        outer_expert,
    )


def solution(mesh):
    placed = (
        P("fsdp", "ctx", None),
        P("fsdp", None),
        P("fsdp", "ctx", None),
        P("fsdp", "ctx", None),
        P(),
        P(("fsdp", "ctx"), None, "tp"),
        P(None, "tp"),
        P("tp", ("fsdp", "ctx")),
        P(),
        P(),
        P(("fsdp", "ctx"), None, "tp"),
        P("tp", ("fsdp", "ctx")),
        P(("fsdp", "ctx"), None, None, "tp"),
        P(("fsdp", "ctx"), "tp", None),
        P("fsdp", "ctx", None),
    )
    plan = eight_plan if mesh.shape["fsdp"] == 4 and mesh.shape["ctx"] == 2 else general_plan
    return jax.shard_map(
        plan,
        mesh=mesh,
        in_specs=placed,
        out_specs=(
            P("fsdp", "ctx", None),
            P("fsdp", "ctx", None),
            P(),
            P(("fsdp", "ctx"), None, "tp"),
            P(None, "tp"),
            P("tp", ("fsdp", "ctx")),
            P(),
            P(),
            P(("fsdp", "ctx"), None, "tp"),
            P("tp", ("fsdp", "ctx")),
            P(("fsdp", "ctx"), None, None, "tp"),
            P(("fsdp", "ctx"), "tp", None),
        ),
        check_vma=False,
    )
```

```python
import math

import jax
import jax.numpy as jnp
from jax import lax
from jax.experimental import pallas as pl
from jax.experimental.pallas import tpu as pltpu
from jax.sharding import PartitionSpec as P

HEAD_DIM = 128
TOP = 4
WINDOW = 1024


rotary_base = 1000000.0
norm_epsilon = 1e-06
masked_score = -1e30


def from_behind(block, axis, distance):
    devices = range(lax.axis_size(axis))
    route = [(i - distance, i) for i in devices if i - distance in devices]
    return lax.ppermute(block, axis, route)


def rotary_tables(positions):
    exponent = jnp.arange(HEAD_DIM // 2, dtype=jnp.float32) * (2.0 / HEAD_DIM)
    inverse = jnp.exp(-math.log(rotary_base) * exponent)
    angle = positions.astype(jnp.float32)[..., None] * inverse
    cosine = jnp.cos(angle)
    sine_table = jnp.sin(angle)
    return (
        jnp.concatenate([cosine, cosine], axis=-1),
        jnp.concatenate([sine_table, sine_table], axis=-1),
    )


def rotate(values, cosine, sine_table):
    half_dim = values.shape[-1] // 2
    turned = jnp.concatenate([-values[..., half_dim:], values[..., :half_dim]], axis=-1)
    return values * cosine + turned * sine_table


def rotate_back(grads, cosine, sine_table):
    half_dim = grads.shape[-1] // 2
    scaled = grads * sine_table
    turned = jnp.concatenate([scaled[..., half_dim:], -scaled[..., :half_dim]], axis=-1)
    return grads * cosine + turned


def document_layout(lengths, positions):
    ends = jnp.cumsum(lengths)
    number = jnp.sum((positions[:, None] >= ends[None, :-1]).astype(jnp.int32), axis=1)
    starts = ends - lengths
    picked = jnp.arange(lengths.shape[0], dtype=jnp.int32)[None, :] == number[:, None]
    first = jnp.sum(jnp.where(picked, starts[None, :], 0), axis=1)
    return (number, positions - first)


def root_norm(values, gain):
    scale = lax.rsqrt(jnp.mean(values * values, axis=-1, keepdims=True) + norm_epsilon)
    return values * scale * gain


def silu_parts(gate_pre):
    sigma = jax.nn.sigmoid(gate_pre)
    return (gate_pre * sigma, sigma * (1.0 + gate_pre * (1.0 - sigma)))


def attend_forward(queries, keys_all, values_all, allowed, score_scale):
    scores = (
        jnp.einsum("qhd,khd->hqk", queries, keys_all, preferred_element_type=jnp.float32)
        * score_scale
    )
    scores = jnp.where(allowed[None], scores, masked_score)
    row_max = jnp.max(scores, axis=-1, keepdims=True)
    row_total = jnp.sum(jnp.exp(scores - row_max), axis=-1, keepdims=True)
    log_total = row_max + jnp.log(row_total)
    weights_low = jnp.exp(scores - log_total).astype(jnp.bfloat16)
    mixed_result = jnp.einsum(
        "hqk,khd->qhd", weights_low, values_all, preferred_element_type=jnp.float32
    )
    return (mixed_result.astype(jnp.bfloat16), log_total)


def attend_backward(queries, keys_all, values_all, allowed, log_total, grad_mixed, score_scale):
    scores = (
        jnp.einsum("qhd,khd->hqk", queries, keys_all, preferred_element_type=jnp.float32)
        * score_scale
    )
    scores = jnp.where(allowed[None], scores, masked_score)
    soft = jnp.exp(scores - log_total)
    grad_soft = jnp.einsum(
        "qhd,khd->hqk", grad_mixed, values_all, preferred_element_type=jnp.float32
    )
    centre = jnp.sum(soft * grad_soft, axis=-1, keepdims=True)
    grad_scores = (soft * (grad_soft - centre)).astype(jnp.bfloat16)
    grad_queries = (
        jnp.einsum("hqk,khd->qhd", grad_scores, keys_all, preferred_element_type=jnp.float32)
        * score_scale
    )
    grad_keys = (
        jnp.einsum("hqk,qhd->khd", grad_scores, queries, preferred_element_type=jnp.float32)
        * score_scale
    )
    grad_values = jnp.einsum(
        "hqk,qhd->khd", soft.astype(jnp.bfloat16), grad_mixed, preferred_element_type=jnp.float32
    )
    return (grad_queries, grad_keys, grad_values)


def general_plan(
    hidden_in,
    doc_lengths,
    expert_ids,
    fill_rank,
    norm_gains,
    qkv_weight,
    qkv_bias,
    out_weight,
    router_weight,
    blend_weight,
    shared_inner,
    shared_outer,
    expert_inner,
    expert_outer,
    cotangent,
):
    seq_count, half_len, width = hidden_in.shape
    tokens = seq_count * half_len
    local_width = qkv_weight.shape[2]
    local_heads = local_width // HEAD_DIM
    experts = router_weight.shape[1]
    expert_local = expert_inner.shape[0]
    groups = experts // expert_local
    capacity = tokens * TOP // experts
    score_scale = 1.0 / math.sqrt(HEAD_DIM)
    gains = norm_gains.astype(jnp.float32)
    qkv_full, out_full, inner_full, outer_full = (
        lax.all_gather(qkv_weight, ("fsdp", "ctx"), axis=0, tiled=True),
        lax.all_gather(out_weight, ("fsdp", "ctx"), axis=1, tiled=True),
        lax.all_gather(shared_inner, ("fsdp", "ctx"), axis=0, tiled=True),
        lax.all_gather(shared_outer, ("fsdp", "ctx"), axis=1, tiled=True),
    )
    positions = lax.axis_index("ctx") * half_len + jnp.arange(half_len, dtype=jnp.int32)
    earlier_pos = positions - half_len
    own_number, own_place = jax.vmap(document_layout, in_axes=(0, None))(doc_lengths, positions)
    prior_number = jax.vmap(document_layout, in_axes=(0, None))(doc_lengths, earlier_pos)[0]
    cosine, sine_table = rotary_tables(own_place)
    cosine = cosine[:, :, None, :]
    sine_table = sine_table[:, :, None, :]
    key_positions = jnp.concatenate([earlier_pos, positions])
    distance = positions[:, None] - key_positions[None, :]
    base_allowed = (distance >= 0) & (distance < WINDOW) & (key_positions[None, :] >= 0)
    key_numbers = jnp.concatenate([prior_number, own_number], axis=1)
    allowed = base_allowed[None] & (own_number[:, :, None] == key_numbers[:, None, :])
    residual = hidden_in.reshape(tokens, width).astype(jnp.float32)
    first_normalized = root_norm(residual, gains[0]).astype(jnp.bfloat16)
    linear_projection = (
        jnp.einsum("td,dcm->tcm", first_normalized, qkv_full, preferred_element_type=jnp.float32)
        + qkv_bias.astype(jnp.float32)[None]
    )
    heads = linear_projection.reshape(seq_count, half_len, 3, local_heads, HEAD_DIM)
    queries = rotate(heads[:, :, 0], cosine, sine_table).astype(jnp.bfloat16)
    keys_own = rotate(heads[:, :, 1], cosine, sine_table).astype(jnp.bfloat16)
    values_own = heads[:, :, 2].astype(jnp.bfloat16)
    keys_prior, values_prior = from_behind((keys_own, values_own), "ctx", 1)
    keys_all = jnp.concatenate([keys_prior, keys_own], axis=1)
    values_all = jnp.concatenate([values_prior, values_own], axis=1)
    sequence = 0
    mixed_one, log_one = attend_forward(
        queries[sequence], keys_all[sequence], values_all[sequence], allowed[sequence], score_scale
    )
    mixed_parts = [mixed_one]
    log_parts = [log_one]
    mixed_result = jnp.stack(mixed_parts).reshape(tokens, local_width)
    attn_part = jnp.dot(mixed_result, out_full, preferred_element_type=jnp.float32)
    after_attn = residual + lax.psum(attn_part, "tp")
    second_normalized = root_norm(after_attn, gains[1]).astype(jnp.bfloat16)
    router_logits = jnp.dot(second_normalized, router_weight, preferred_element_type=jnp.float32)
    router_probs = jax.nn.softmax(router_logits, axis=-1)
    route_rows = expert_ids.reshape(tokens, TOP)
    onehot = (route_rows[:, :, None] == jnp.arange(experts, dtype=jnp.int32)[None, None, :]).astype(
        jnp.float32
    )
    gate_values = jnp.sum(onehot * router_probs[:, None, :], axis=-1)
    membership = jnp.sum(onehot, axis=1).astype(jnp.bfloat16)
    priority = fill_rank.reshape(tokens)
    earlier = (priority[None, :] < priority[:, None]).astype(jnp.bfloat16)
    slot_counts = jnp.dot(earlier, membership, preferred_element_type=jnp.float32)
    slot_index = jnp.sum(onehot * slot_counts[:, None, :], axis=-1).astype(jnp.int32)
    kept_pairs = slot_index < capacity
    keep_weight = kept_pairs.astype(jnp.float32)
    flat_index = route_rows * capacity + slot_index
    target = jnp.where(kept_pairs, flat_index, experts * capacity).reshape(-1)
    pair_index = jnp.where(kept_pairs, flat_index, 0)
    token_ids = jnp.broadcast_to(
        jnp.arange(tokens, dtype=jnp.int32)[:, None], (tokens, TOP)
    ).reshape(-1)
    source = jnp.zeros((experts * capacity,), jnp.int32).at[target].set(token_ids, mode="drop")
    filled = jnp.zeros((experts * capacity,), jnp.bool_).at[target].set(True, mode="drop")
    slot_gate = (
        jnp.zeros((experts * capacity,), jnp.float32)
        .at[target]
        .set(gate_values.reshape(-1), mode="drop")
    )
    dispatch = jnp.where(filled[:, None], second_normalized[source], jnp.zeros((), jnp.bfloat16))
    expert_rows = lax.all_to_all(
        dispatch.reshape(groups, expert_local, capacity, width),
        ("fsdp", "ctx"),
        split_axis=0,
        concat_axis=2,
        tiled=True,
    )[0]
    expert_pre = jnp.einsum(
        "erd,edgf->ergf", expert_rows, expert_inner, preferred_element_type=jnp.float32
    )
    expert_act, expert_slope = silu_parts(expert_pre[:, :, 0])
    expert_hidden = (expert_act * expert_pre[:, :, 1]).astype(jnp.bfloat16)
    expert_result = jnp.einsum(
        "erf,efd->erd", expert_hidden, expert_outer, preferred_element_type=jnp.float32
    )
    returned = (
        lax.all_to_all(
            expert_result[None].astype(jnp.bfloat16),
            ("fsdp", "ctx"),
            split_axis=2,
            concat_axis=0,
            tiled=True,
        )
        .astype(jnp.float32)
        .reshape(experts * capacity, width)
    )
    common_expert_preactivation = jnp.einsum(
        "td,dgf->tgf", second_normalized, inner_full, preferred_element_type=jnp.float32
    )
    shared_act, shared_slope = silu_parts(common_expert_preactivation[:, 0])
    common_expert_hidden = (shared_act * common_expert_preactivation[:, 1]).astype(jnp.bfloat16)
    shared_part = jnp.dot(common_expert_hidden, outer_full, preferred_element_type=jnp.float32)
    blend = jax.nn.sigmoid(
        jnp.dot(second_normalized, blend_weight, preferred_element_type=jnp.float32)
    )
    expert_part = jnp.zeros((tokens, width), jnp.float32)
    for route_slot in range(TOP):
        expert_part = (
            expert_part
            + (keep_weight[:, route_slot] * gate_values[:, route_slot])[:, None]
            * returned[pair_index[:, route_slot]]
        )
    branch = lax.psum(
        (blend[:, None] * shared_part + expert_part).astype(jnp.bfloat16), "tp"
    ).astype(jnp.float32)
    layer_out = (after_attn + branch).astype(jnp.bfloat16).reshape(seq_count, half_len, width)
    grad_y = cotangent.reshape(tokens, width).astype(jnp.float32)
    shared_dot = jnp.sum(grad_y * shared_part, axis=-1)
    gate_dots = []
    for route_slot in range(TOP):
        gate_dots.append(jnp.sum(grad_y * returned[pair_index[:, route_slot]], axis=-1))
    gate_dot = jnp.stack(gate_dots, axis=1)
    grad_shared = (blend[:, None] * grad_y).astype(jnp.bfloat16)
    grad_shared_hidden = jnp.einsum(
        "td,fd->tf", grad_shared, outer_full, preferred_element_type=jnp.float32
    )
    grad_shared_pre = jnp.stack(
        [
            grad_shared_hidden * common_expert_preactivation[:, 1] * shared_slope,
            grad_shared_hidden * shared_act,
        ],
        axis=1,
    ).astype(jnp.bfloat16)
    inner_grad_full = jnp.einsum(
        "td,tgf->dgf", second_normalized, grad_shared_pre, preferred_element_type=jnp.float32
    )
    outer_grad_full = jnp.einsum(
        "tf,td->fd", common_expert_hidden, grad_shared, preferred_element_type=jnp.float32
    )
    grad_normed_part = jnp.einsum(
        "tgf,dgf->td", grad_shared_pre, inner_full, preferred_element_type=jnp.float32
    )
    grad_result = jnp.where(filled[:, None], slot_gate[:, None] * grad_y[source], 0.0).astype(
        jnp.bfloat16
    )
    grad_rows_in = lax.all_to_all(
        grad_result.reshape(groups, expert_local, capacity, width),
        ("fsdp", "ctx"),
        split_axis=0,
        concat_axis=2,
        tiled=True,
    )[0]
    grad_expert_hidden = jnp.einsum(
        "erd,efd->erf", grad_rows_in, expert_outer, preferred_element_type=jnp.float32
    )
    grad_expert_pre = jnp.stack(
        [grad_expert_hidden * expert_pre[:, :, 1] * expert_slope, grad_expert_hidden * expert_act],
        axis=2,
    ).astype(jnp.bfloat16)
    outer_expert = jnp.einsum(
        "erf,erd->efd", expert_hidden, grad_rows_in, preferred_element_type=jnp.float32
    )
    inner_expert = jnp.einsum(
        "erd,ergf->edgf", expert_rows, grad_expert_pre, preferred_element_type=jnp.float32
    )
    grad_rows_out = jnp.einsum(
        "ergf,edgf->erd", grad_expert_pre, expert_inner, preferred_element_type=jnp.float32
    )
    returned_back = (
        lax.all_to_all(
            grad_rows_out[None].astype(jnp.bfloat16),
            ("fsdp", "ctx"),
            split_axis=2,
            concat_axis=0,
            tiled=True,
        )
        .astype(jnp.float32)
        .reshape(experts * capacity, width)
    )
    for route_slot in range(TOP):
        grad_normed_part = (
            grad_normed_part
            + keep_weight[:, route_slot][:, None] * returned_back[pair_index[:, route_slot]]
        )
    grad_normed_sum, shared_total, gate_total = lax.psum(
        (grad_normed_part, shared_dot, gate_dot), "tp"
    )
    grad_blend = (blend * (1.0 - blend) * shared_total).astype(jnp.bfloat16)
    grad_gate = keep_weight * gate_total
    grad_probs = jnp.sum(onehot * grad_gate[:, :, None], axis=1)
    grad_logits = (
        router_probs * (grad_probs - jnp.sum(router_probs * grad_probs, axis=-1, keepdims=True))
    ).astype(jnp.bfloat16)
    router_grad_part = jnp.einsum(
        "td,te->de", second_normalized, grad_logits, preferred_element_type=jnp.float32
    )
    blend_grad_part = jnp.einsum(
        "td,t->d", second_normalized, grad_blend, preferred_element_type=jnp.float32
    )
    grad_normed_two = (
        grad_normed_sum
        + jnp.einsum("te,de->td", grad_logits, router_weight, preferred_element_type=jnp.float32)
        + grad_blend.astype(jnp.float32)[:, None] * blend_weight.astype(jnp.float32)[None, :]
    )
    after_norm_grad, gain_two_grad = jax.vjp(root_norm, after_attn, gains[1])[1](grad_normed_two)
    grad_after = grad_y + after_norm_grad
    grad_attn = grad_after.astype(jnp.bfloat16)
    projection_full = jnp.einsum(
        "tm,td->md", mixed_result, grad_attn, preferred_element_type=jnp.float32
    )
    grad_mixed = (
        jnp.einsum("td,md->tm", grad_attn, out_full, preferred_element_type=jnp.float32)
        .astype(jnp.bfloat16)
        .reshape(seq_count, half_len, local_heads, HEAD_DIM)
    )
    sequence = 0
    grad_query, grad_key, grad_value = attend_backward(
        queries[sequence],
        keys_all[sequence],
        values_all[sequence],
        allowed[sequence],
        log_parts[sequence],
        grad_mixed[sequence],
        score_scale,
    )
    query_parts = [grad_query]
    key_parts = [grad_key]
    value_parts = [grad_value]
    grad_queries = jnp.stack(query_parts)
    grad_keys = jnp.stack(key_parts)
    grad_values = jnp.stack(value_parts)
    sent_keys, sent_values = (
        from_behind(grad_keys[:, :half_len].astype(jnp.bfloat16), "ctx", -1).astype(jnp.float32),
        from_behind(grad_values[:, :half_len].astype(jnp.bfloat16), "ctx", -1).astype(jnp.float32),
    )
    grad_keys_own = grad_keys[:, half_len:] + sent_keys
    grad_values_own = grad_values[:, half_len:] + sent_values
    grad_linear = (
        jnp.stack(
            [
                rotate_back(grad_queries, cosine, sine_table),
                rotate_back(grad_keys_own, cosine, sine_table),
                grad_values_own,
            ],
            axis=2,
        )
        .astype(jnp.bfloat16)
        .reshape(tokens, 3, local_width)
    )
    bias_part = jnp.sum(grad_linear.astype(jnp.float32), axis=0)
    qkv_grad_full = jnp.einsum(
        "td,tcm->dcm", first_normalized, grad_linear, preferred_element_type=jnp.float32
    )
    grad_normed_one = lax.psum(
        jnp.einsum("tcm,dcm->td", grad_linear, qkv_full, preferred_element_type=jnp.float32).astype(
            jnp.bfloat16
        ),
        "tp",
    ).astype(jnp.float32)
    residual_norm_grad, gain_one_grad = jax.vjp(root_norm, residual, gains[0])[1](grad_normed_one)
    input_grad = (
        (grad_after + residual_norm_grad).astype(jnp.bfloat16).reshape(seq_count, half_len, width)
    )
    qkv_grad, projection_grad, inner_shared, outer_shared = (
        lax.psum_scatter(
            qkv_grad_full.astype(jnp.bfloat16), ("fsdp", "ctx"), scatter_dimension=0, tiled=True
        ).astype(jnp.float32),
        lax.psum_scatter(
            projection_full.astype(jnp.bfloat16), ("fsdp", "ctx"), scatter_dimension=1, tiled=True
        ).astype(jnp.float32),
        lax.psum_scatter(
            inner_grad_full.astype(jnp.bfloat16), ("fsdp", "ctx"), scatter_dimension=0, tiled=True
        ).astype(jnp.float32),
        lax.psum_scatter(
            outer_grad_full.astype(jnp.bfloat16), ("fsdp", "ctx"), scatter_dimension=1, tiled=True
        ).astype(jnp.float32),
    )
    gains_grad, bias_grad, router_grad, blend_grad = (
        lax.psum(
            jnp.stack([gain_one_grad, gain_two_grad]).astype(jnp.bfloat16), ("fsdp", "ctx")
        ).astype(jnp.float32),
        lax.psum(bias_part.astype(jnp.bfloat16), ("fsdp", "ctx")).astype(jnp.float32),
        lax.psum(router_grad_part.astype(jnp.bfloat16), ("fsdp", "ctx")).astype(jnp.float32),
        lax.psum(blend_grad_part.astype(jnp.bfloat16), ("fsdp", "ctx")).astype(jnp.float32),
    )
    return (
        layer_out,
        input_grad,
        gains_grad,
        qkv_grad,
        bias_grad,
        projection_grad,
        router_grad,
        blend_grad,
        inner_shared,
        outer_shared,
        inner_expert,
        outer_expert,
    )


VMEM = pl.BlockSpec(memory_space=pltpu.VMEM)
SMEM = pl.BlockSpec(memory_space=pltpu.SMEM)
ANY = pl.BlockSpec(memory_space=pl.ANY)
ROWS_COLS = (((1,), (0,)), ((), ()))
ROWS_ROWS = (((1,), (1,)), ((), ()))
COLS_COLS = (((0,), (0,)), ((), ()))


def product(one, other, dims=ROWS_COLS):
    return lax.dot_general(one, other, dims, preferred_element_type=jnp.float32)


def call(kernel, shapes, flops, moved, **others):
    return pl.pallas_call(
        kernel,
        out_shape=shapes,
        compiler_params=pltpu.CompilerParams(vmem_limit_bytes=40 * 2**20),
        cost_estimate=pl.CostEstimate(
            flops=int(flops), bytes_accessed=int(moved), transcendentals=0
        ),
        **others,
    )


def after(values, *earlier):
    return lax.optimization_barrier((values, earlier))[0]


def swap_x(values):
    return lax.ppermute(values, "fsdp", [(f, f ^ 2) for f in range(4)])


def swap_core(values):
    return lax.ppermute(values, "fsdp", [(f, f ^ 1) for f in range(4)])


def swap_y(values):
    return lax.ppermute(values, "ctx", [(0, 1), (1, 0)])


def own_number():
    return lax.axis_index("fsdp") * 2 + lax.axis_index("ctx")


def exchange_order(parts):
    number = own_number()
    for bit in (4, 2, 1):
        taken = (number & bit) != 0
        parts = [jnp.where(taken, parts[i ^ bit], parts[i]) for i in range(8)]
    return parts


def add_low(one, other):
    return (one.astype(jnp.float32) + other.astype(jnp.float32)).astype(jnp.bfloat16)


def halves_sum(own, arrived):
    half = own.shape[0] // 2
    return add_low(own[:half], arrived[:half]), add_low(own[half:], arrived[half:])


def first_hops(taken):
    return swap_x(taken[1][0]), swap_y(taken[2][1]), swap_x(taken[3][0]), swap_y(taken[3][1])


def last_hops(taken, hops):
    _, _, both_low, both_high = hops
    for_x, for_y = add_low(taken[1][1], both_high), add_low(taken[2][0], both_low)
    return swap_x(for_x), swap_y(for_y)


def hops_sum(taken, hops, ends):
    x_low, y_high, _, _ = hops
    x_high, y_low = ends
    sums = [
        mine.astype(jnp.float32) + along_x.astype(jnp.float32) + along_y.astype(jnp.float32)
        for mine, along_x, along_y in ((taken[0][0], x_low, y_low), (taken[0][1], x_high, y_high))
    ]
    return jnp.concatenate(sums).astype(jnp.bfloat16)


def sum_over(values, with_tp):
    values = values + swap_core(values)
    values = values + swap_x(values)
    values = values + swap_y(values)
    if with_tp:
        count = lax.axis_size("tp")
        bit = 1
        while bit < count:
            values = values + lax.ppermute(values, "tp", [(i, i ^ bit) for i in range(count)])
            bit *= 2
    return values


def line_reduce(rows):
    count = lax.axis_size("tp")
    blocks = rows.reshape((count, rows.shape[0] // count) + rows.shape[1:])
    arrived = lax.all_to_all(blocks, "tp", split_axis=0, concat_axis=0, tiled=True)
    return jnp.sum(arrived.astype(jnp.float32), axis=0)


def line_gather(block):
    copies = jnp.broadcast_to(block[None], (lax.axis_size("tp"),) + block.shape)
    return lax.all_to_all(copies, "tp", split_axis=0, concat_axis=0, tiled=True)


def pick(blocks, index):
    return lax.dynamic_index_in_dim(blocks, index, axis=0, keepdims=False)


def hop_reduce(rows):
    count = lax.axis_size("tp")
    me = lax.axis_index("tp")
    blocks = rows.reshape((count, rows.shape[0] // count) + rows.shape[1:])
    right, left = None, None
    for step in range(1, count):
        to_right = pick(blocks, jnp.minimum(count - step + me, count - 1))
        to_left = pick(blocks, jnp.maximum(step + me - count, 0))
        if step > 1:
            to_right, to_left = add_low(to_right, right), add_low(to_left, left)
        right = lax.ppermute(to_right, "tp", [(i, i + 1) for i in range(min(step, count - 1))])
        left = lax.ppermute(
            to_left, "tp", [(i, i - 1) for i in range(max(count - step, 1), count)]
        )
    return (
        pick(blocks, me).astype(jnp.float32)
        + right.astype(jnp.float32)
        + left.astype(jnp.float32)
    )


def hop_gather(block):
    count = lax.axis_size("tp")
    me = lax.axis_index("tp")
    right, left = [block], [block]
    for step in range(1, count):
        right.append(
            lax.ppermute(right[-1], "tp", [(i, i + 1) for i in range(step - 1, count - 1)])
        )
        left.append(
            lax.ppermute(left[-1], "tp", [(i, i - 1) for i in range(1, count - step + 1)])
        )
    result = []
    for place in range(count):
        taken = block
        for step in range(1, count):
            taken = jnp.where(place == me - step, right[step], taken)
            taken = jnp.where(place == me + step, left[step], taken)
        result.append(taken)
    return jnp.concatenate(result)


def hop_trade(parts):
    rows = parts[0].shape[0]
    from_y = swap_y(jnp.concatenate([parts[1], parts[3]]))
    from_x = swap_x(jnp.concatenate([parts[4], parts[6]]))
    both = lax.ppermute(
        jnp.concatenate([parts[5], parts[7]]),
        ("fsdp", "ctx"),
        [(d, d ^ 5) for d in range(8)],
    )
    sibling = swap_core(
        jnp.concatenate([parts[2], from_y[rows:], from_x[rows:], both[rows:]])
    )
    return [
        parts[0],
        from_y[:rows],
        sibling[:rows],
        sibling[rows : 2 * rows],
        from_x[:rows],
        both[:rows],
        sibling[2 * rows : 3 * rows],
        sibling[3 * rows :],
    ]


def columns_of(values, count):
    wide = values.shape[1] // count
    return [values[:, i * wide : (i + 1) * wide] for i in range(count)]


def block_columns(index, wide):
    return pl.ds(pl.multiple_of(index * wide, wide), wide)


def turn(values, cosine, signed_sine):
    return values * cosine + pltpu.roll(values, HEAD_DIM // 2, 1) * signed_sine


def pieces_of(lists):
    flat, places = [], []
    for pieces in lists:
        places.append(range(len(flat), len(flat) + len(pieces)))
        flat += pieces
    return flat, places


def project(number, hidden, gain, weights, bias, cosine, signed_sine):
    tokens, width = hidden.shape
    local_width = bias.shape[2]
    deep = width // 8

    flat, places = pieces_of(weights)

    def kernel(number_ref, hidden_ref, gain_ref, bias_ref, cos_ref, sin_ref, *others):
        weight_refs, (out_ref, normed_ref) = others[: len(flat)], others[len(flat) :]
        part = pl.program_id(0)

        @pl.when(part == 0)
        def _():
            values = hidden_ref[...].astype(jnp.float32)
            normed_ref[...] = root_norm(values, gain_ref[...]).astype(jnp.bfloat16)

        total = None
        for r in range(8):
            rows = normed_ref[:, block_columns(number_ref[0] ^ r, deep)]
            terms = [product(rows, weight_refs[at][0]) for at in places[r]]
            term = terms[0] if len(terms) == 1 else jnp.concatenate(terms, axis=1)
            total = term if total is None else total + term
        total = total + bias_ref[0]
        cosine_now = jnp.where(part < 2, cos_ref[...], 1.0)
        sine_now = jnp.where(part < 2, sin_ref[...], 0.0)
        for h in range(local_width // HEAD_DIM):
            at = slice(h * HEAD_DIM, (h + 1) * HEAD_DIM)
            out_ref[0, :, at] = turn(total[:, at], cosine_now, sine_now).astype(jnp.bfloat16)

    whole = lambda *shape: pl.BlockSpec(shape, lambda c: (0,) * len(shape))
    return call(
        kernel,
        [
            jax.ShapeDtypeStruct((3, tokens, local_width), jnp.bfloat16),
            jax.ShapeDtypeStruct((tokens, width), jnp.bfloat16),
        ],
        2 * tokens * width * 3 * local_width,
        2 * (2 * tokens * width + 3 * width * local_width + 3 * tokens * local_width),
        grid=(3,),
        in_specs=[
            SMEM,
            whole(tokens, width),
            whole(1, width),
            pl.BlockSpec((1, 1, local_width), lambda c: (c, 0, 0)),
            whole(tokens, HEAD_DIM),
            whole(tokens, HEAD_DIM),
        ]
        + [pl.BlockSpec((1,) + piece.shape[1:], lambda c: (c, 0, 0)) for piece in flat],
        out_specs=[
            pl.BlockSpec((1, tokens, local_width), lambda c: (c, 0, 0)),
            whole(tokens, width),
        ],
    )(number, hidden, gain, bias, cosine, signed_sine, *flat)


ATTEND_ROWS = 176


def attend(projected, prior, masks, score_scale):
    _, tokens, local_width = projected.shape
    heads = local_width // HEAD_DIM
    tiles = tokens // ATTEND_ROWS

    def kernel(q_ref, own_ref, prior_ref, mask_own_ref, mask_prior_ref, mixed_ref, log_ref):
        for h in range(heads):
            at = slice(h * HEAD_DIM, (h + 1) * HEAD_DIM)
            queries = q_ref[0, :, at]
            score_own = product(queries, own_ref[1, :, at], ROWS_ROWS) * score_scale
            score_own = score_own + mask_own_ref[...]
            score_prior = product(queries, prior_ref[0, :, at], ROWS_ROWS) * score_scale
            score_prior = score_prior + mask_prior_ref[...]
            row_max = jnp.maximum(
                jnp.max(score_own, axis=-1, keepdims=True),
                jnp.max(score_prior, axis=-1, keepdims=True),
            )
            own = jnp.exp(score_own - row_max)
            before = jnp.exp(score_prior - row_max)
            total = jnp.sum(own, axis=-1, keepdims=True) + jnp.sum(before, axis=-1, keepdims=True)
            scale = 1.0 / total
            mixed = product((own * scale).astype(jnp.bfloat16), own_ref[2, :, at])
            mixed = mixed + product((before * scale).astype(jnp.bfloat16), prior_ref[1, :, at])
            mixed_ref[:, at] = mixed.astype(jnp.bfloat16)
            log_ref[:, h : h + 1] = row_max + jnp.log(total)

    return call(
        kernel,
        [
            jax.ShapeDtypeStruct((tokens, local_width), jnp.bfloat16),
            jax.ShapeDtypeStruct((tokens, heads), jnp.float32),
        ],
        8 * tokens * tokens * local_width,
        8 * tokens * tokens + 12 * tokens * local_width,
        grid=(tiles,),
        in_specs=[
            pl.BlockSpec((1, ATTEND_ROWS, local_width), lambda i: (0, i, 0)),
            pl.BlockSpec((3, tokens, local_width), lambda i: (0, 0, 0)),
            pl.BlockSpec((2, tokens, local_width), lambda i: (0, 0, 0)),
            pl.BlockSpec((ATTEND_ROWS, tokens), lambda i: (i, 0)),
            pl.BlockSpec((ATTEND_ROWS, tokens), lambda i: (i, 0)),
        ],
        out_specs=[
            pl.BlockSpec((ATTEND_ROWS, local_width), lambda i: (i, 0)),
            pl.BlockSpec((ATTEND_ROWS, heads), lambda i: (i, 0)),
        ],
    )(projected, projected, prior, *masks)


def attend_back(projected, prior, masks, log_total, grad_mixed, cosine, signed_sine, score_scale):
    _, tokens, local_width = projected.shape
    heads = local_width // HEAD_DIM
    tiles = tokens // ATTEND_ROWS

    def kernel(
        q_ref, own_ref, prior_ref, mask_own_ref, mask_prior_ref, log_ref, grad_ref, cos_ref, sin_ref,
        query_out, own_out, prior_out, own_sum, prior_sum,
    ):
        tile = pl.program_id(0)

        @pl.when(tile == 0)
        def _():
            own_sum[...] = jnp.zeros_like(own_sum)
            prior_sum[...] = jnp.zeros_like(prior_sum)

        for h in range(heads):
            at = slice(h * HEAD_DIM, (h + 1) * HEAD_DIM)
            queries = q_ref[0, :, at]
            grads = grad_ref[:, at]
            log_now = log_ref[:, h : h + 1]
            soft, low, dots = [], [], []
            for keys, values, mask_ref in (
                (own_ref[1, :, at], own_ref[2, :, at], mask_own_ref),
                (prior_ref[0, :, at], prior_ref[1, :, at], mask_prior_ref),
            ):
                score = product(queries, keys, ROWS_ROWS) * score_scale + mask_ref[...]
                soft.append(jnp.exp(score - log_now))
                dots.append(product(grads, values, ROWS_ROWS))
            centre = jnp.sum(soft[0] * dots[0], axis=-1, keepdims=True)
            centre = centre + jnp.sum(soft[1] * dots[1], axis=-1, keepdims=True)
            grad_query = None
            for side, sums, keys in (
                (0, own_sum, own_ref[1, :, at]),
                (1, prior_sum, prior_ref[0, :, at]),
            ):
                grad_score = (soft[side] * (dots[side] - centre)).astype(jnp.bfloat16)
                term = product(grad_score, keys)
                grad_query = term if grad_query is None else grad_query + term
                sums[0, :, at] += product(grad_score, queries, COLS_COLS)
                sums[1, :, at] += product(soft[side].astype(jnp.bfloat16), grads, COLS_COLS)
            query_out[:, at] = turn(
                grad_query * score_scale, cos_ref[...], -sin_ref[...]
            ).astype(jnp.bfloat16)

        @pl.when(tile == tiles - 1)
        def _():
            own_out[0] = own_sum[0] * score_scale
            own_out[1] = own_sum[1]
            prior_out[0] = (prior_sum[0] * score_scale).astype(jnp.bfloat16)
            prior_out[1] = prior_sum[1].astype(jnp.bfloat16)

    row_block = lambda wide: pl.BlockSpec((ATTEND_ROWS, wide), lambda i: (i, 0))
    whole = lambda *shape: pl.BlockSpec(shape, lambda i: (0,) * len(shape))
    pair = (2, tokens, local_width)
    return call(
        kernel,
        [
            jax.ShapeDtypeStruct((tokens, local_width), jnp.bfloat16),
            jax.ShapeDtypeStruct(pair, jnp.float32),
            jax.ShapeDtypeStruct(pair, jnp.bfloat16),
        ],
        20 * tokens * tokens * local_width,
        8 * tokens * tokens + 30 * tokens * local_width,
        grid=(tiles,),
        in_specs=[
            pl.BlockSpec((1, ATTEND_ROWS, local_width), lambda i: (0, i, 0)),
            whole(3, tokens, local_width),
            whole(2, tokens, local_width),
            row_block(tokens),
            row_block(tokens),
            row_block(heads),
            row_block(local_width),
            row_block(HEAD_DIM),
            row_block(HEAD_DIM),
        ],
        out_specs=[row_block(local_width), whole(*pair), whole(*pair)],
        scratch_shapes=[pltpu.VMEM(pair, jnp.float32), pltpu.VMEM(pair, jnp.float32)],
    )(projected, projected, prior, *masks, log_total, grad_mixed, cosine, signed_sine)


def project_back(number, grad_query, grad_own, arrived, cosine, signed_sine, hidden, weights):
    tokens, local_width = grad_query.shape
    flat, places = pieces_of(weights)
    deep = flat[0].shape[1]
    width = 8 * deep
    rows = tokens // 2

    def kernel(number_ref, query_ref, own_ref, arrived_ref, cos_ref, sin_ref, hidden_ref, *others):
        weight_refs = others[: len(flat)]
        linear_ref, bias_ref, gain_ref, out_ref = others[len(flat) :]

        @pl.when(pl.program_id(0) == 0)
        def _():
            bias_ref[...] = jnp.zeros_like(bias_ref)
            gain_ref[...] = jnp.zeros_like(gain_ref)

        residual = hidden_ref[...].astype(jnp.float32)
        scale = lax.rsqrt(jnp.mean(residual * residual, axis=-1, keepdims=True) + norm_epsilon)

        keys = own_ref[0] + arrived_ref[0].astype(jnp.float32)
        linear_ref[0] = query_ref[...]
        for h in range(local_width // HEAD_DIM):
            at = slice(h * HEAD_DIM, (h + 1) * HEAD_DIM)
            linear_ref[1, :, at] = turn(keys[:, at], cos_ref[...], -sin_ref[...]).astype(
                jnp.bfloat16
            )
        linear_ref[2] = (own_ref[1] + arrived_ref[1].astype(jnp.float32)).astype(jnp.bfloat16)
        for c in range(3):
            bias_ref[c] += jnp.sum(linear_ref[c].astype(jnp.float32), axis=0, keepdims=True)
        for r in range(8):
            total = None
            for c in range(3):
                first = 0
                for at in places[r]:
                    last = first + flat[at].shape[2]
                    term = product(linear_ref[c, :, first:last], weight_refs[at][c], ROWS_ROWS)
                    total = term if total is None else total + term
                    first = last
            columns = block_columns(number_ref[0] ^ r, deep)
            out_ref[:, columns] = total.astype(jnp.bfloat16)
            scaled = hidden_ref[:, columns].astype(jnp.float32) * scale
            gain_ref[:, columns] += jnp.sum(total * scaled, axis=0, keepdims=True)

    whole = lambda *shape: pl.BlockSpec(shape, lambda i: (0,) * len(shape))
    row_block = lambda wide: pl.BlockSpec((rows, wide), lambda i: (i, 0))
    pair_block = pl.BlockSpec((2, rows, local_width), lambda i: (0, i, 0))
    return call(
        kernel,
        [
            jax.ShapeDtypeStruct((3, tokens, local_width), jnp.bfloat16),
            jax.ShapeDtypeStruct((3, 1, local_width), jnp.float32),
            jax.ShapeDtypeStruct((1, width), jnp.float32),
            jax.ShapeDtypeStruct((tokens, width), jnp.bfloat16),
        ],
        6 * tokens * local_width * width,
        2 * (tokens * width + 3 * width * local_width + 12 * tokens * local_width),
        grid=(2,),
        in_specs=[
            SMEM,
            row_block(local_width),
            pair_block,
            pair_block,
            row_block(HEAD_DIM),
            row_block(HEAD_DIM),
            row_block(width),
        ]
        + [whole(*piece.shape) for piece in flat],
        out_specs=[
            pl.BlockSpec((3, rows, local_width), lambda i: (0, i, 0)),
            whole(3, 1, local_width),
            whole(1, width),
            row_block(width),
        ],
    )(number, grad_query, grad_own, arrived, cosine, signed_sine, hidden, *flat)


def project_weights(normed, grad_linear):
    tokens, width = normed.shape
    local_width = grad_linear.shape[2]
    deep = width // 8

    def kernel(normed_ref, linear_ref, out_ref):
        columns = block_columns(pl.program_id(0), deep)
        for c in range(3):
            out_ref[0, c] = product(normed_ref[:, columns], linear_ref[c], COLS_COLS).astype(
                jnp.bfloat16
            )

    whole = lambda *shape: pl.BlockSpec(shape, lambda i: (0,) * len(shape))
    return call(
        kernel,
        jax.ShapeDtypeStruct((8, 3, deep, local_width), jnp.bfloat16),
        6 * tokens * local_width * width,
        2 * (tokens * width + 3 * width * local_width + 3 * tokens * local_width),
        grid=(8,),
        in_specs=[whole(tokens, width), whole(3, tokens, local_width)],
        out_specs=pl.BlockSpec((1, 3, deep, local_width), lambda i: (i, 0, 0, 0)),
    )(normed, grad_linear)


def lay_weights(expert_t, expert_outer, shared_rows, router_rows, pad):
    _, hid_e, width = expert_t.shape
    hid_s = shared_rows.shape[0] // 3
    hid = hid_e + hid_s
    last = hid + router_rows.shape[0]

    def kernel(expert_ref, outer_ref, shared_ref, router_ref, inner_out, outer_out):
        zeros = jnp.zeros((pad - hid, width), jnp.bfloat16)
        inner_out[:hid_e] = expert_ref[0]
        inner_out[hid_e:hid] = shared_ref[:hid_s]
        inner_out[hid:last] = router_ref[...]
        inner_out[last:pad] = zeros[: pad - last]
        inner_out[pad : pad + hid_e] = expert_ref[1]
        inner_out[pad + hid_e : pad + hid] = shared_ref[hid_s : 2 * hid_s]
        inner_out[pad + hid :] = zeros
        outer_out[:hid_e] = outer_ref[...]
        outer_out[hid_e:hid] = shared_ref[2 * hid_s :]
        outer_out[hid:] = zeros

    return call(
        kernel,
        [
            jax.ShapeDtypeStruct((2 * pad, width), jnp.bfloat16),
            jax.ShapeDtypeStruct((pad, width), jnp.bfloat16),
        ],
        0,
        12 * pad * width,
        in_specs=[VMEM] * 4,
        out_specs=[VMEM] * 2,
    )(expert_t, expert_outer, shared_rows, router_rows)


MIX_ROWS = 352
LANES = 128


def tiles_of(pieces):
    return [(at, first) for at, p in enumerate(pieces) for first in range(0, p.shape[0], MIX_ROWS)]


def next_tile(refs, starts, buffer, sems):
    tile = pl.program_id(0)

    def copy(number):
        at, first = starts[number]
        return pltpu.make_async_copy(
            refs[at].at[pl.ds(first, MIX_ROWS)], buffer.at[number % 2], sems.at[number % 2]
        )

    for number in range(len(starts)):

        @pl.when(tile == number)
        def _():
            if number == 0:
                copy(0).start()
            if number + 1 < len(starts):
                copy(number + 1).start()
            copy(number).wait()

    return buffer[lax.rem(tile, 2)]


def narrow(pieces, other):
    starts = tiles_of(pieces)
    units, width = other.shape

    def kernel(other_ref, *refs):
        piece_refs, (out_ref, buffer, sems) = refs[: len(pieces)], refs[len(pieces) :]
        rows = next_tile(piece_refs, starts, buffer, sems)
        out_ref[...] = product(rows, other_ref[...], ROWS_ROWS)

    tokens = len(starts) * MIX_ROWS
    return call(
        kernel,
        jax.ShapeDtypeStruct((tokens, units), jnp.float32),
        2 * tokens * units * width,
        2 * (tokens * width + units * width + 2 * tokens * units),
        grid=(len(starts),),
        in_specs=[pl.BlockSpec((units, width), lambda i: (0, 0))] + [ANY] * len(pieces),
        out_specs=pl.BlockSpec((MIX_ROWS, units), lambda i: (i, 0)),
        scratch_shapes=[
            pltpu.VMEM((2, MIX_ROWS, width), jnp.bfloat16),
            pltpu.SemaphoreType.DMA((2,)),
        ],
    )(other, *pieces)


def widen(parts, other):
    starts = tiles_of(parts)
    units, width = other.shape
    rows = parts[0].shape[0] // 2
    each = rows // MIX_ROWS
    count = 2 * len(parts)

    def kernel(other_ref, *refs):
        part_refs = refs[: len(parts)]
        outs, (buffer, sems) = refs[len(parts) : len(parts) + count], refs[len(parts) + count :]
        value = product(next_tile(part_refs, starts, buffer, sems), other_ref[...])
        for at in range(count):

            @pl.when(pl.program_id(0) // each == at)
            def _():
                outs[at][...] = value.astype(jnp.bfloat16)

    def place(at):
        return pl.BlockSpec(
            (MIX_ROWS, width), lambda i: (jnp.clip(i - at * each, 0, each - 1), 0)
        )

    tokens = count * rows
    return call(
        kernel,
        [jax.ShapeDtypeStruct((rows, width), jnp.bfloat16)] * count,
        2 * tokens * units * width,
        2 * (tokens * width + units * width + tokens * units),
        grid=(len(starts),),
        in_specs=[pl.BlockSpec((units, width), lambda i: (0, 0))] + [ANY] * len(parts),
        out_specs=[place(at) for at in range(count)],
        scratch_shapes=[
            pltpu.VMEM((2, MIX_ROWS, units), jnp.bfloat16),
            pltpu.SemaphoreType.DMA((2,)),
        ],
    )(other, *parts)


def mixture(row_pieces, upstream, kept, mine, inner, hid_e, hid, experts):
    tokens, pad = upstream.shape
    width = inner.shape[1]
    starts = tiles_of(row_pieces)
    tiles = len(starts)
    count = len(row_pieces)
    first_router = hid - (pad - LANES)

    def kernel(kept_ref, mine_ref, inner_ref, upstream_ref, *others):
        row_refs = others[:count]
        pre_out, weighted_out, other_out, own_out, buffer, sems = others[count:]
        tile = pl.program_id(0)
        rows = next_tile(row_refs, starts, buffer, sems)
        pre = product(rows, inner_ref[...], ROWS_ROWS)
        upstream = upstream_ref[...]
        gate_pre, up_pre = pre[:, :pad], pre[:, pad:]
        tail = gate_pre[:, pad - LANES :]
        lane = lax.broadcasted_iota(jnp.int32, tail.shape, 1) - first_router
        routed = (lane >= 0) & (lane < experts)
        logits = jnp.where(routed, tail, -1e30)
        raised = jnp.exp(logits - jnp.max(logits, axis=-1, keepdims=True))
        probs = raised / jnp.sum(raised, axis=-1, keepdims=True)
        own_prob = jnp.sum(probs * mine_ref[...], axis=-1, keepdims=True)
        blend = jax.nn.sigmoid(
            jnp.sum(jnp.where(lane == experts, tail, 0.0), axis=-1, keepdims=True)
        )
        kept_now = kept_ref[...]
        of_expert = lax.broadcasted_iota(jnp.int32, gate_pre.shape, 1) < hid_e
        weight = jnp.where(of_expert, kept_now * own_prob, blend)
        sigma = jax.nn.sigmoid(gate_pre)
        act = gate_pre * sigma
        slope = sigma + act * (1.0 - sigma)
        hidden = (act * up_pre).astype(jnp.bfloat16).astype(jnp.float32)
        inner_dot = hidden * upstream
        gate_dot = jnp.sum(jnp.where(of_expert, inner_dot, 0.0), axis=-1, keepdims=True)
        blend_dot = jnp.sum(jnp.where(of_expert, 0.0, inner_dot), axis=-1, keepdims=True)
        grad_router = probs * (kept_now * gate_dot) * (mine_ref[...] - own_prob)
        grad_blend = blend * (1.0 - blend) * blend_dot
        scaled = weight * upstream
        grad_gate = scaled * up_pre * slope
        grad_tail = grad_gate[:, pad - LANES :] + jnp.where(
            lane == experts, grad_blend, grad_router
        )
        pre_out[:, : pad - LANES] = grad_gate[:, : pad - LANES].astype(jnp.bfloat16)
        pre_out[:, pad - LANES : pad] = grad_tail.astype(jnp.bfloat16)
        pre_out[:, pad:] = (scaled * act).astype(jnp.bfloat16)
        weighted_out[...] = (weight * hidden).astype(jnp.bfloat16)
        back = product(pre_out[...], inner_ref[...]).astype(jnp.bfloat16)

        @pl.when(tile < tiles // 2)
        def _():
            other_out[...] = back

        @pl.when(tile >= tiles // 2)
        def _():
            own_out[...] = back

    whole = lambda *shape: pl.BlockSpec(shape, lambda i: (0,) * len(shape))
    row_block = lambda wide: pl.BlockSpec((MIX_ROWS, wide), lambda i: (i, 0))
    half = jax.ShapeDtypeStruct((tokens // 2, width), jnp.bfloat16)
    return call(
        kernel,
        [
            jax.ShapeDtypeStruct((tokens, 2 * pad), jnp.bfloat16),
            jax.ShapeDtypeStruct((tokens, pad), jnp.bfloat16),
            half,
            half,
        ],
        8 * tokens * pad * width,
        2 * (2 * tokens * width + 5 * tokens * pad + 2 * pad * width),
        grid=(tiles,),
        in_specs=[row_block(1), whole(1, LANES), whole(2 * pad, width), row_block(pad)]
        + [ANY] * count,
        out_specs=[
            row_block(2 * pad),
            row_block(pad),
            pl.BlockSpec((MIX_ROWS, width), lambda i: (jnp.minimum(i, tiles // 2 - 1), 0)),
            pl.BlockSpec((MIX_ROWS, width), lambda i: (jnp.maximum(i - tiles // 2, 0), 0)),
        ],
        scratch_shapes=[
            pltpu.VMEM((2, MIX_ROWS, width), jnp.bfloat16),
            pltpu.SemaphoreType.DMA((2,)),
        ],
    )(kept, mine, inner, upstream, *row_pieces)


def attend_out(numbers, hidden, gain, mixed, own_weights, other_weights):
    tokens, width = hidden.shape
    count, _, local_width = mixed.shape
    deep = own_weights[0].shape[1]
    long = count * local_width
    rows = tokens // count

    def kernel(numbers_ref, hidden_ref, gain_ref, mixed_ref, *others):
        own_refs, (other_ref, normed_ref, kept_ref, sum_ref) = others[:4], others[4:]
        heads = jnp.concatenate([mixed_ref[i] for i in range(count)], axis=1)
        for r in range(8):
            chip = (r // 4) * 2 + r % 2
            if (r // 2) % 2:
                weight = other_ref[chip * long : (chip + 1) * long]
            else:
                weight = own_refs[chip][...]
            columns = block_columns(numbers_ref[0] ^ r, deep)
            sum_ref[:, columns] = hidden_ref[:, columns].astype(jnp.float32) + product(
                heads, weight
            )
        values = sum_ref[...]
        normed_ref[...] = root_norm(values, gain_ref[...]).astype(jnp.bfloat16)

        @pl.when(pl.program_id(0) == numbers_ref[1])
        def _():
            kept_ref[...] = values

    whole = lambda *shape: pl.BlockSpec(shape, lambda i: (0,) * len(shape))
    row_block = lambda wide: pl.BlockSpec((rows, wide), lambda i: (i, 0))
    return call(
        kernel,
        [
            jax.ShapeDtypeStruct((tokens, width), jnp.bfloat16),
            jax.ShapeDtypeStruct((rows, width), jnp.float32),
        ],
        2 * tokens * width * long,
        2 * (3 * tokens * width + long * width),
        grid=(count,),
        in_specs=[
            SMEM,
            row_block(width),
            whole(1, width),
            pl.BlockSpec((count, rows, local_width), lambda i: (0, i, 0)),
        ]
        + [whole(long, deep)] * 4
        + [whole(4 * long, deep)],
        out_specs=[row_block(width), whole(rows, width)],
        scratch_shapes=[pltpu.VMEM((rows, width), jnp.float32)],
    )(numbers, hidden, gain, mixed, *own_weights, other_weights)


def attend_out_back(numbers, grads, own_weights, other_weights, count):
    rows, width = grads.shape
    long, deep = own_weights[0].shape
    local_width = long // count

    def kernel(numbers_ref, grads_ref, *others):
        own_refs, (other_ref, mixed_ref) = others[:4], others[4:]
        for i in range(count):
            total = None
            for r in range(8):
                chip = (r // 4) * 2 + r % 2
                first = i * local_width
                if (r // 2) % 2:
                    weight = other_ref[chip * long + first : chip * long + first + local_width]
                else:
                    weight = own_refs[chip][first : first + local_width]
                taken = grads_ref[:, block_columns(numbers_ref[0] ^ r, deep)]
                term = product(taken, weight, ROWS_ROWS)
                total = term if total is None else total + term
            mixed_ref[i] = total.astype(jnp.bfloat16)

    whole = lambda *shape: pl.BlockSpec(shape, lambda i: (0,) * len(shape))
    return call(
        kernel,
        jax.ShapeDtypeStruct((count, rows, local_width), jnp.bfloat16),
        2 * rows * width * long,
        2 * (2 * rows * width + long * width),
        grid=(1,),
        in_specs=[SMEM, whole(rows, width)] + [whole(long, deep)] * 4 + [whole(4 * long, deep)],
        out_specs=whole(count, rows, local_width),
    )(numbers, grads, *own_weights, other_weights)


def weight_gradients(parts, row_pieces, tile):
    units = parts[0].shape[1]
    width = row_pieces[0][0].shape[1]
    tokens = parts[0].shape[0]
    pieces = [piece for chip in row_pieces for piece in chip]
    firsts = [sum(p.shape[0] for p in pieces[:i]) for i in range(len(pieces))]
    chips = len(parts)

    def kernel(*refs):
        part_refs, piece_refs = refs[:chips], refs[chips : chips + len(pieces)]
        out_ref, buffer, sems = refs[chips + len(pieces) :]
        copies = [
            pltpu.make_async_copy(
                ref, buffer.at[pl.ds(firsts[i], pieces[i].shape[0])], sems.at[i]
            )
            for i, ref in enumerate(piece_refs)
        ]

        @pl.when(pl.program_id(0) == 0)
        def _():
            for copy in copies:
                copy.start()
            for copy in copies:
                copy.wait()

        total = None
        for chip in range(chips):
            rows = buffer[chip * tokens : (chip + 1) * tokens]
            term = product(part_refs[chip][...], rows, COLS_COLS)
            total = term if total is None else total + term
        out_ref[...] = total

    return call(
        kernel,
        jax.ShapeDtypeStruct((units, width), jnp.float32),
        2 * chips * tokens * units * width,
        2 * chips * tokens * (units + width) + 4 * units * width,
        grid=(units // tile,),
        in_specs=[pl.BlockSpec((tokens, tile), lambda i: (0, i))] * chips + [ANY] * len(pieces),
        out_specs=pl.BlockSpec((tile, width), lambda i: (i, 0)),
        scratch_shapes=[
            pltpu.VMEM((chips * tokens, width), jnp.bfloat16),
            pltpu.SemaphoreType.DMA((len(pieces),)),
        ],
    )(*parts, *pieces)


def eight_plan(
    hidden_in,
    doc_lengths,
    expert_ids,
    fill_rank,
    norm_gains,
    qkv_weight,
    qkv_bias,
    out_weight,
    router_weight,
    blend_weight,
    shared_inner,
    shared_outer,
    expert_inner,
    expert_outer,
    cotangent,
):
    _, tokens, width = hidden_in.shape
    local_width = qkv_weight.shape[2]
    experts = router_weight.shape[1]
    capacity = tokens * TOP // experts
    score_scale = 1.0 / math.sqrt(HEAD_DIM)
    gains = norm_gains.astype(jnp.float32)
    me_tp = lax.axis_index("tp")
    tp = lax.axis_size("tp")
    share = tokens // tp
    number = own_number()
    numbers = jnp.stack([number, me_tp])
    deep = width // 8
    half_width = local_width // 2

    def own_rows(values):
        return lax.dynamic_slice_in_dim(values, me_tp * share, share, axis=0)

    def own_columns(heads):
        return lax.dynamic_slice_in_dim(heads, me_tp * share, share, axis=1)

    qkv_own = jnp.transpose(qkv_weight, (1, 0, 2))
    qkv_x, qkv_y = swap_x(qkv_own), swap_y(qkv_own)
    qkv_sibling = swap_core(qkv_own)
    out_line = lax.all_gather(out_weight, "tp", axis=0, tiled=True)

    route_rows = expert_ids.reshape(tokens, TOP)
    named = jnp.sum(
        (route_rows[:, :, None] == jnp.arange(experts, dtype=jnp.int32)[None, None, :]).astype(
            jnp.float32
        ),
        axis=1,
    )
    priority = fill_rank.reshape(tokens)
    earlier = (priority[None, :] < priority[:, None]).astype(jnp.bfloat16)
    slot_counts = jnp.dot(
        earlier, named.astype(jnp.bfloat16), preferred_element_type=jnp.float32
    )
    kept_all = named * (slot_counts < capacity).astype(jnp.float32)
    kept_blocks = lax.all_to_all(
        kept_all.T.reshape(experts, 1, tokens),
        ("fsdp", "ctx"),
        split_axis=0,
        concat_axis=0,
        tiled=True,
    )

    positions = lax.axis_index("ctx") * tokens + jnp.arange(tokens, dtype=jnp.int32)
    earlier_pos = positions - tokens
    doc_number, doc_place = document_layout(doc_lengths[0], positions)
    prior_number = document_layout(doc_lengths[0], earlier_pos)[0]
    cosine, sine_table = rotary_tables(doc_place)
    half_dim = HEAD_DIM // 2
    signed_sine = jnp.concatenate([-sine_table[:, :half_dim], sine_table[:, half_dim:]], axis=1)
    masks = []
    for places, doc_numbers in ((positions, doc_number), (earlier_pos, prior_number)):
        distance = positions[:, None] - places[None, :]
        allowed = (
            (distance >= 0)
            & (distance < WINDOW)
            & (places[None, :] >= 0)
            & (doc_number[:, None] == doc_numbers[None, :])
        )
        masks.append(jnp.where(allowed, 0.0, masked_score))

    shared_t = jnp.transpose(shared_inner, (1, 2, 0))
    hid_s = shared_t.shape[1] // 8
    to_trade = jnp.concatenate(
        [
            shared_t.reshape(2, 8, hid_s, deep)[0],
            shared_t.reshape(2, 8, hid_s, deep)[1],
            shared_outer.reshape(8, hid_s, deep),
        ],
        axis=1,
    )

    (qkv_x, qkv_y), early_kept = after((qkv_x, qkv_y), kept_all), kept_blocks
    qkv_low = swap_x(qkv_y[:, :, :half_width])
    qkv_high = swap_y(qkv_x[:, :, half_width:])
    qkv_parts = [
        [qkv_own],
        [qkv_y],
        [qkv_sibling],
        [swap_core(qkv_y)],
        [qkv_x],
        [qkv_low, qkv_high],
        [swap_core(qkv_x)],
        [swap_core(qkv_low), swap_core(qkv_high)],
    ]
    hidden_rows = hidden_in.reshape(tokens, width)
    hidden_first, (cosine, signed_sine), masks = after(
        (hidden_rows, (cosine, signed_sine), masks), early_kept
    )
    projected, first_normalized = project(
        numbers,
        hidden_first,
        gains[:1],
        qkv_parts,
        qkv_bias.astype(jnp.float32)[:, None],
        cosine,
        signed_sine,
    )
    prior = from_behind(projected[1:], "ctx", 1)

    grad_rows = cotangent.reshape(tokens, width)
    grads_share = after(own_rows(grad_rows), qkv_low, qkv_high)
    grads_x, grads_y = swap_x(grads_share), swap_y(grads_share)
    grads_both = lax.ppermute(grads_share, ("fsdp", "ctx"), [(d, d ^ 5) for d in range(8)])
    grads_x, grads_y, grads_both = after((grads_x, grads_y, grads_both), projected)
    grads_x = line_gather(grads_x).reshape(tokens, width)

    out_own = after(out_line, qkv_low, qkv_high)
    out_x = swap_x(out_own)

    prior = after(prior, grads_y, grads_both)
    mixed_result, log_total = attend(projected, prior, masks, score_scale)
    mixed_all = line_gather(after(mixed_result, grads_x))

    to_trade, out_late = after((to_trade, out_own), mixed_result)
    out_y = swap_y(out_late)
    out_both = swap_x(out_y)
    traded = hop_trade(exchange_order([to_trade[d] for d in range(8)]))
    out_mine = [out_own, out_y, out_x, out_both]
    out_other = swap_core(after(jnp.concatenate(out_mine), mixed_result))
    grads_sibling = swap_core(after(grad_rows, projected))
    hidden_rows = hidden_in.reshape(tokens, width)

    kept_rel = exchange_order([kept_blocks[i].reshape(tokens, 1) for i in range(8)])
    kept_chips = [jnp.concatenate([kept_rel[p + 2], kept_rel[p]]) for p in (0, 4, 1, 5)]
    shared_rows = jnp.concatenate(exchange_order(after(traded, mixed_result)), axis=1)
    hid_e = expert_inner.shape[3]
    hid = hid_e + hid_s
    router_rows = jnp.concatenate(
        [
            router_weight.T,
            blend_weight[None],
            jnp.zeros((-(experts + 1) % 16, width), jnp.bfloat16),
        ]
    )
    pad = -(-(hid + router_rows.shape[0]) // LANES) * LANES
    inner, outer = lay_weights(
        jnp.transpose(expert_inner[0], (1, 2, 0)),
        expert_outer[0],
        shared_rows,
        router_rows,
        pad,
    )
    mine = (
        jnp.arange(LANES, dtype=jnp.int32) == number + (hid - (pad - LANES))
    ).astype(jnp.float32)[None]
    grad_chips = [[grads_sibling, grad_rows], [swap_core(grads_x), grads_x]]
    upstream = [narrow(grad_chips[0], outer)]
    upstream.append(narrow(after(grad_chips[1], upstream[0]), outer))
    mixed_all, upstream = after((mixed_all, upstream))
    second_normalized, after_own = attend_out(
        numbers, hidden_rows, gains[1:], mixed_all, out_mine, out_other
    )
    grads_y = line_gather(after(grads_y, second_normalized)).reshape(tokens, width)
    rows_x, rows_y = swap_x(second_normalized), swap_y(second_normalized)
    row_chips = [[swap_core(second_normalized), second_normalized]]

    def mix(chip, *earlier):
        return mixture(
            row_chips[chip],
            upstream[chip],
            after(kept_chips[chip], earlier),
            mine,
            inner,
            hid_e,
            hid,
            experts,
        )

    mixes = [mix(0)]
    back_arrived = [swap_core(mixes[0][2])]
    rows_x, rows_y = after((rows_x, rows_y), mixes[0][0])
    rows_low = swap_x(rows_y[: tokens // 2])
    rows_high = swap_y(rows_x[tokens // 2 :])
    row_chips += [[swap_core(rows_x), rows_x], [swap_core(rows_y), rows_y]]
    grads_y = after(grads_y, mixes[0][0])
    grad_chips.append([swap_core(grads_y), grads_y])
    grads_both = line_gather(after(grads_both, grads_y)).reshape(tokens, width)
    upstream.append(narrow(grad_chips[2], outer))
    mixes.append(mix(1, upstream[2]))
    back_arrived.append(swap_core(mixes[1][2]))
    rows_low, rows_high = after((rows_low, rows_high), mixes[1][0])
    mixes.append(mix(2, back_arrived[0], rows_low, rows_high))
    back_arrived.append(swap_core(mixes[2][2]))
    taken = [halves_sum(mixes[chip][3], back_arrived[chip]) for chip in range(2)]
    x_low = swap_x(taken[1][0])
    row_chips.append([swap_core(rows_low), swap_core(rows_high), rows_low, rows_high])
    grads_both = after(grads_both, mixes[1][0])
    grad_chips.append([swap_core(grads_both), grads_both])
    upstream.append(narrow(after(grad_chips[3], mixes[2][0], taken), outer))
    taken.append(halves_sum(mixes[2][3], after(back_arrived[2], upstream[3])))
    y_high = swap_y(taken[2][1])
    mixes.append(mix(3, taken[2], row_chips[3]))
    back_arrived.append(swap_core(after(mixes[3][2], x_low, y_high)))
    taken.append(halves_sum(mixes[3][3], back_arrived[3]))
    hops = [x_low, y_high, swap_x(taken[3][0]), swap_y(taken[3][1])]

    pre_list = [m[0] for m in mixes]
    weighted_list = after([m[1] for m in mixes], taken[3])
    forward = widen(weighted_list, outer)
    hops = after(hops, forward)
    ends = last_hops(taken, hops)
    forward = after(forward, hops)
    arrived_forward = [swap_core(forward[2 * chip]) for chip in range(4)]
    forward_taken = [halves_sum(forward[2 * c + 1], arrived_forward[c]) for c in range(4)]
    back_sum = hops_sum(taken, hops, after(ends, forward_taken))
    grad_normed_two = line_reduce(back_sum)
    forward_hops = first_hops(after(forward_taken, back_sum))
    outer_grad = weight_gradients(after(weighted_list, back_sum), grad_chips, LANES)
    inner_grad = weight_gradients(after(pre_list, outer_grad), row_chips, 256)
    grad_normed_two, forward_hops = after((grad_normed_two, forward_hops), inner_grad)
    forward_ends = last_hops(forward_taken, forward_hops)

    grad_y = own_rows(grad_rows).astype(jnp.float32)
    after_norm_grad, gain_two_grad = jax.vjp(root_norm, after_own, gains[1])[1](grad_normed_two)
    grad_after = grad_y + after_norm_grad
    grad_attn = grad_after.astype(jnp.bfloat16)

    grad_heads = attend_out_back(numbers, grad_attn, out_mine, out_other, tp)
    grad_mixed = lax.all_to_all(
        grad_heads, "tp", split_axis=0, concat_axis=0, tiled=True
    ).reshape(tokens, local_width)
    heads_own = after(own_columns(mixed_all), grad_heads)
    projection_full = lax.dot_general(
        heads_own, grad_attn, (((1,), (0,)), ((), ())), preferred_element_type=jnp.float32
    ).astype(jnp.bfloat16)
    projection_grad = lax.psum_scatter(
        projection_full.reshape(tp * local_width, width),
        ("fsdp", "ctx"),
        scatter_dimension=1,
        tiled=True,
    )
    projection_grad = lax.psum_scatter(
        projection_grad, "tp", scatter_dimension=0, tiled=True
    ).astype(jnp.float32)

    grad_mixed, forward_ends = after((grad_mixed, forward_ends))
    forward_sum = hops_sum(forward_taken, forward_hops, forward_ends)
    grad_query, grad_own, grad_prior = attend_back(
        projected, prior, masks, log_total, grad_mixed, cosine, signed_sine, score_scale
    )
    arrived = from_behind(grad_prior, "ctx", -1)
    layer_own = after_own + hop_reduce(after(forward_sum, grad_prior))
    shared_grad = jnp.concatenate(
        [inner_grad[hid_e:hid], inner_grad[pad + hid_e : pad + hid], outer_grad[hid_e:hid]]
    ).astype(jnp.bfloat16)
    shared_parts = exchange_order(columns_of(after(shared_grad, grad_mixed), 8))
    shared_parts = hop_trade(after(shared_parts, grad_prior))
    arrived, layer_own, shared_parts = after((arrived, layer_own, shared_parts))
    grad_linear, bias_part, gain_one_part, grad_one_part = project_back(
        numbers, grad_query, grad_own, arrived, cosine, signed_sine, hidden_rows, qkv_parts
    )
    grad_normed_one = hop_reduce(grad_one_part)
    residual_own = own_rows(hidden_rows).astype(jnp.float32)
    residual_norm_grad, _ = jax.vjp(root_norm, residual_own, gains[0])[1](grad_normed_one)
    input_own = (grad_after + residual_norm_grad).astype(jnp.bfloat16)
    input_grad = line_gather(input_own).reshape(1, tokens, width)
    layer_out = hop_gather(after(layer_own.astype(jnp.bfloat16), grad_one_part))
    input_grad = after(input_grad, layer_out)
    layer_out = layer_out.reshape(1, tokens, width)

    grad_linear, late = after((grad_linear, grad_normed_one), grad_one_part)
    qkv_full = project_weights(first_normalized, grad_linear)
    qkv_grad = jnp.transpose(
        lax.psum_scatter(
            qkv_full.reshape(8 * 3 * deep, local_width),
            ("fsdp", "ctx"),
            scatter_dimension=0,
            tiled=True,
        ).reshape(3, deep, local_width),
        (1, 0, 2),
    ).astype(jnp.float32)

    inner_grad, outer_grad = after((inner_grad, outer_grad), late)
    inner_expert = jnp.transpose(
        jnp.stack([inner_grad[:hid_e], inner_grad[pad : pad + hid_e]]), (2, 0, 1)
    )[None]
    outer_expert = outer_grad[:hid_e][None]
    shared_back = jnp.stack(exchange_order(after(shared_parts, late)))
    inner_shared = jnp.transpose(
        jnp.stack([shared_back[:, :hid_s], shared_back[:, hid_s : 2 * hid_s]]).reshape(
            2, 8 * hid_s, deep
        ),
        (2, 0, 1),
    ).astype(jnp.float32)
    outer_shared = shared_back[:, 2 * hid_s :].reshape(8 * hid_s, deep).astype(jnp.float32)

    small = sum_over(
        jnp.concatenate(
            [
                inner_grad[hid : hid + experts + 1],
                after(gain_one_part, late),
                gain_two_grad[None],
            ]
        ),
        True,
    )
    router_grad = small[:experts].T
    blend_grad = small[experts]
    gains_grad = small[experts + 1 :]
    bias_grad = sum_over(after(bias_part, late).reshape(3, local_width), False)
    return (
        layer_out,
        input_grad,
        gains_grad,
        qkv_grad,
        bias_grad,
        projection_grad,
        router_grad,
        blend_grad,
        inner_shared,
        outer_shared,
        inner_expert,
        outer_expert,
    )


def solution(mesh):
    placed = (
        P("fsdp", "ctx", None),
        P("fsdp", None),
        P("fsdp", "ctx", None),
        P("fsdp", "ctx", None),
        P(),
        P(("fsdp", "ctx"), None, "tp"),
        P(None, "tp"),
        P("tp", ("fsdp", "ctx")),
        P(),
        P(),
        P(("fsdp", "ctx"), None, "tp"),
        P("tp", ("fsdp", "ctx")),
        P(("fsdp", "ctx"), None, None, "tp"),
        P(("fsdp", "ctx"), "tp", None),
        P("fsdp", "ctx", None),
    )
    plan = eight_plan if mesh.shape["fsdp"] == 4 and mesh.shape["ctx"] == 2 else general_plan
    return jax.shard_map(
        plan,
        mesh=mesh,
        in_specs=placed,
        out_specs=(
            P("fsdp", "ctx", None),
            P("fsdp", "ctx", None),
            P(),
            P(("fsdp", "ctx"), None, "tp"),
            P(None, "tp"),
            P("tp", ("fsdp", "ctx")),
            P(),
            P(),
            P(("fsdp", "ctx"), None, "tp"),
            P("tp", ("fsdp", "ctx")),
            P(("fsdp", "ctx"), None, None, "tp"),
            P(("fsdp", "ctx"), "tp", None),
        ),
        check_vma=False,
    )
```

```python
import math

import jax
import jax.numpy as jnp
from jax import lax
from jax.experimental import pallas as pl
from jax.experimental.pallas import tpu as pltpu
from jax.sharding import PartitionSpec as P

HEAD_DIM = 128
TOP = 4
WINDOW = 1024


rotary_base = 1000000.0
norm_epsilon = 1e-06
masked_score = -1e30


def from_behind(block, axis, distance):
    devices = range(lax.axis_size(axis))
    route = [(i - distance, i) for i in devices if i - distance in devices]
    return lax.ppermute(block, axis, route)


def rotary_tables(positions):
    exponent = jnp.arange(HEAD_DIM // 2, dtype=jnp.float32) * (2.0 / HEAD_DIM)
    inverse = jnp.exp(-math.log(rotary_base) * exponent)
    angle = positions.astype(jnp.float32)[..., None] * inverse
    cosine = jnp.cos(angle)
    sine_table = jnp.sin(angle)
    return (
        jnp.concatenate([cosine, cosine], axis=-1),
        jnp.concatenate([sine_table, sine_table], axis=-1),
    )


def rotate(values, cosine, sine_table):
    half_dim = values.shape[-1] // 2
    turned = jnp.concatenate([-values[..., half_dim:], values[..., :half_dim]], axis=-1)
    return values * cosine + turned * sine_table


def rotate_back(grads, cosine, sine_table):
    half_dim = grads.shape[-1] // 2
    scaled = grads * sine_table
    turned = jnp.concatenate([scaled[..., half_dim:], -scaled[..., :half_dim]], axis=-1)
    return grads * cosine + turned


def document_layout(lengths, positions):
    ends = jnp.cumsum(lengths)
    number = jnp.sum((positions[:, None] >= ends[None, :-1]).astype(jnp.int32), axis=1)
    starts = ends - lengths
    picked = jnp.arange(lengths.shape[0], dtype=jnp.int32)[None, :] == number[:, None]
    first = jnp.sum(jnp.where(picked, starts[None, :], 0), axis=1)
    return (number, positions - first)


def root_norm(values, gain):
    scale = lax.rsqrt(jnp.mean(values * values, axis=-1, keepdims=True) + norm_epsilon)
    return values * scale * gain


def silu_parts(gate_pre):
    sigma = jax.nn.sigmoid(gate_pre)
    return (gate_pre * sigma, sigma * (1.0 + gate_pre * (1.0 - sigma)))


def attend_forward(queries, keys_all, values_all, allowed, score_scale):
    scores = (
        jnp.einsum("qhd,khd->hqk", queries, keys_all, preferred_element_type=jnp.float32)
        * score_scale
    )
    scores = jnp.where(allowed[None], scores, masked_score)
    row_max = jnp.max(scores, axis=-1, keepdims=True)
    row_total = jnp.sum(jnp.exp(scores - row_max), axis=-1, keepdims=True)
    log_total = row_max + jnp.log(row_total)
    weights_low = jnp.exp(scores - log_total).astype(jnp.bfloat16)
    mixed_result = jnp.einsum(
        "hqk,khd->qhd", weights_low, values_all, preferred_element_type=jnp.float32
    )
    return (mixed_result.astype(jnp.bfloat16), log_total)


def attend_backward(queries, keys_all, values_all, allowed, log_total, grad_mixed, score_scale):
    scores = (
        jnp.einsum("qhd,khd->hqk", queries, keys_all, preferred_element_type=jnp.float32)
        * score_scale
    )
    scores = jnp.where(allowed[None], scores, masked_score)
    soft = jnp.exp(scores - log_total)
    grad_soft = jnp.einsum(
        "qhd,khd->hqk", grad_mixed, values_all, preferred_element_type=jnp.float32
    )
    centre = jnp.sum(soft * grad_soft, axis=-1, keepdims=True)
    grad_scores = (soft * (grad_soft - centre)).astype(jnp.bfloat16)
    grad_queries = (
        jnp.einsum("hqk,khd->qhd", grad_scores, keys_all, preferred_element_type=jnp.float32)
        * score_scale
    )
    grad_keys = (
        jnp.einsum("hqk,qhd->khd", grad_scores, queries, preferred_element_type=jnp.float32)
        * score_scale
    )
    grad_values = jnp.einsum(
        "hqk,qhd->khd", soft.astype(jnp.bfloat16), grad_mixed, preferred_element_type=jnp.float32
    )
    return (grad_queries, grad_keys, grad_values)


def general_plan(
    hidden_in,
    doc_lengths,
    expert_ids,
    fill_rank,
    norm_gains,
    qkv_weight,
    qkv_bias,
    out_weight,
    router_weight,
    blend_weight,
    shared_inner,
    shared_outer,
    expert_inner,
    expert_outer,
    cotangent,
):
    seq_count, half_len, width = hidden_in.shape
    tokens = seq_count * half_len
    local_width = qkv_weight.shape[2]
    local_heads = local_width // HEAD_DIM
    experts = router_weight.shape[1]
    expert_local = expert_inner.shape[0]
    groups = experts // expert_local
    capacity = tokens * TOP // experts
    score_scale = 1.0 / math.sqrt(HEAD_DIM)
    gains = norm_gains.astype(jnp.float32)
    qkv_full, out_full, inner_full, outer_full = (
        lax.all_gather(qkv_weight, ("fsdp", "ctx"), axis=0, tiled=True),
        lax.all_gather(out_weight, ("fsdp", "ctx"), axis=1, tiled=True),
        lax.all_gather(shared_inner, ("fsdp", "ctx"), axis=0, tiled=True),
        lax.all_gather(shared_outer, ("fsdp", "ctx"), axis=1, tiled=True),
    )
    positions = lax.axis_index("ctx") * half_len + jnp.arange(half_len, dtype=jnp.int32)
    earlier_pos = positions - half_len
    own_number, own_place = jax.vmap(document_layout, in_axes=(0, None))(doc_lengths, positions)
    prior_number = jax.vmap(document_layout, in_axes=(0, None))(doc_lengths, earlier_pos)[0]
    cosine, sine_table = rotary_tables(own_place)
    cosine = cosine[:, :, None, :]
    sine_table = sine_table[:, :, None, :]
    key_positions = jnp.concatenate([earlier_pos, positions])
    distance = positions[:, None] - key_positions[None, :]
    base_allowed = (distance >= 0) & (distance < WINDOW) & (key_positions[None, :] >= 0)
    key_numbers = jnp.concatenate([prior_number, own_number], axis=1)
    allowed = base_allowed[None] & (own_number[:, :, None] == key_numbers[:, None, :])
    residual = hidden_in.reshape(tokens, width).astype(jnp.float32)
    first_normalized = root_norm(residual, gains[0]).astype(jnp.bfloat16)
    linear_projection = (
        jnp.einsum("td,dcm->tcm", first_normalized, qkv_full, preferred_element_type=jnp.float32)
        + qkv_bias.astype(jnp.float32)[None]
    )
    heads = linear_projection.reshape(seq_count, half_len, 3, local_heads, HEAD_DIM)
    queries = rotate(heads[:, :, 0], cosine, sine_table).astype(jnp.bfloat16)
    keys_own = rotate(heads[:, :, 1], cosine, sine_table).astype(jnp.bfloat16)
    values_own = heads[:, :, 2].astype(jnp.bfloat16)
    keys_prior, values_prior = from_behind((keys_own, values_own), "ctx", 1)
    keys_all = jnp.concatenate([keys_prior, keys_own], axis=1)
    values_all = jnp.concatenate([values_prior, values_own], axis=1)
    sequence = 0
    mixed_one, log_one = attend_forward(
        queries[sequence], keys_all[sequence], values_all[sequence], allowed[sequence], score_scale
    )
    mixed_parts = [mixed_one]
    log_parts = [log_one]
    mixed_result = jnp.stack(mixed_parts).reshape(tokens, local_width)
    attn_part = jnp.dot(mixed_result, out_full, preferred_element_type=jnp.float32)
    after_attn = residual + lax.psum(attn_part, "tp")
    second_normalized = root_norm(after_attn, gains[1]).astype(jnp.bfloat16)
    router_logits = jnp.dot(second_normalized, router_weight, preferred_element_type=jnp.float32)
    router_probs = jax.nn.softmax(router_logits, axis=-1)
    route_rows = expert_ids.reshape(tokens, TOP)
    onehot = (route_rows[:, :, None] == jnp.arange(experts, dtype=jnp.int32)[None, None, :]).astype(
        jnp.float32
    )
    gate_values = jnp.sum(onehot * router_probs[:, None, :], axis=-1)
    membership = jnp.sum(onehot, axis=1).astype(jnp.bfloat16)
    priority = fill_rank.reshape(tokens)
    earlier = (priority[None, :] < priority[:, None]).astype(jnp.bfloat16)
    slot_counts = jnp.dot(earlier, membership, preferred_element_type=jnp.float32)
    slot_index = jnp.sum(onehot * slot_counts[:, None, :], axis=-1).astype(jnp.int32)
    kept_pairs = slot_index < capacity
    keep_weight = kept_pairs.astype(jnp.float32)
    flat_index = route_rows * capacity + slot_index
    target = jnp.where(kept_pairs, flat_index, experts * capacity).reshape(-1)
    pair_index = jnp.where(kept_pairs, flat_index, 0)
    token_ids = jnp.broadcast_to(
        jnp.arange(tokens, dtype=jnp.int32)[:, None], (tokens, TOP)
    ).reshape(-1)
    source = jnp.zeros((experts * capacity,), jnp.int32).at[target].set(token_ids, mode="drop")
    filled = jnp.zeros((experts * capacity,), jnp.bool_).at[target].set(True, mode="drop")
    slot_gate = (
        jnp.zeros((experts * capacity,), jnp.float32)
        .at[target]
        .set(gate_values.reshape(-1), mode="drop")
    )
    dispatch = jnp.where(filled[:, None], second_normalized[source], jnp.zeros((), jnp.bfloat16))
    expert_rows = lax.all_to_all(
        dispatch.reshape(groups, expert_local, capacity, width),
        ("fsdp", "ctx"),
        split_axis=0,
        concat_axis=2,
        tiled=True,
    )[0]
    expert_pre = jnp.einsum(
        "erd,edgf->ergf", expert_rows, expert_inner, preferred_element_type=jnp.float32
    )
    expert_act, expert_slope = silu_parts(expert_pre[:, :, 0])
    expert_hidden = (expert_act * expert_pre[:, :, 1]).astype(jnp.bfloat16)
    expert_result = jnp.einsum(
        "erf,efd->erd", expert_hidden, expert_outer, preferred_element_type=jnp.float32
    )
    returned = (
        lax.all_to_all(
            expert_result[None].astype(jnp.bfloat16),
            ("fsdp", "ctx"),
            split_axis=2,
            concat_axis=0,
            tiled=True,
        )
        .astype(jnp.float32)
        .reshape(experts * capacity, width)
    )
    common_expert_preactivation = jnp.einsum(
        "td,dgf->tgf", second_normalized, inner_full, preferred_element_type=jnp.float32
    )
    shared_act, shared_slope = silu_parts(common_expert_preactivation[:, 0])
    common_expert_hidden = (shared_act * common_expert_preactivation[:, 1]).astype(jnp.bfloat16)
    shared_part = jnp.dot(common_expert_hidden, outer_full, preferred_element_type=jnp.float32)
    blend = jax.nn.sigmoid(
        jnp.dot(second_normalized, blend_weight, preferred_element_type=jnp.float32)
    )
    expert_part = jnp.zeros((tokens, width), jnp.float32)
    for route_slot in range(TOP):
        expert_part = (
            expert_part
            + (keep_weight[:, route_slot] * gate_values[:, route_slot])[:, None]
            * returned[pair_index[:, route_slot]]
        )
    branch = lax.psum(
        (blend[:, None] * shared_part + expert_part).astype(jnp.bfloat16), "tp"
    ).astype(jnp.float32)
    layer_out = (after_attn + branch).astype(jnp.bfloat16).reshape(seq_count, half_len, width)
    grad_y = cotangent.reshape(tokens, width).astype(jnp.float32)
    shared_dot = jnp.sum(grad_y * shared_part, axis=-1)
    gate_dots = []
    for route_slot in range(TOP):
        gate_dots.append(jnp.sum(grad_y * returned[pair_index[:, route_slot]], axis=-1))
    gate_dot = jnp.stack(gate_dots, axis=1)
    grad_shared = (blend[:, None] * grad_y).astype(jnp.bfloat16)
    grad_shared_hidden = jnp.einsum(
        "td,fd->tf", grad_shared, outer_full, preferred_element_type=jnp.float32
    )
    grad_shared_pre = jnp.stack(
        [
            grad_shared_hidden * common_expert_preactivation[:, 1] * shared_slope,
            grad_shared_hidden * shared_act,
        ],
        axis=1,
    ).astype(jnp.bfloat16)
    inner_grad_full = jnp.einsum(
        "td,tgf->dgf", second_normalized, grad_shared_pre, preferred_element_type=jnp.float32
    )
    outer_grad_full = jnp.einsum(
        "tf,td->fd", common_expert_hidden, grad_shared, preferred_element_type=jnp.float32
    )
    grad_normed_part = jnp.einsum(
        "tgf,dgf->td", grad_shared_pre, inner_full, preferred_element_type=jnp.float32
    )
    grad_result = jnp.where(filled[:, None], slot_gate[:, None] * grad_y[source], 0.0).astype(
        jnp.bfloat16
    )
    grad_rows_in = lax.all_to_all(
        grad_result.reshape(groups, expert_local, capacity, width),
        ("fsdp", "ctx"),
        split_axis=0,
        concat_axis=2,
        tiled=True,
    )[0]
    grad_expert_hidden = jnp.einsum(
        "erd,efd->erf", grad_rows_in, expert_outer, preferred_element_type=jnp.float32
    )
    grad_expert_pre = jnp.stack(
        [grad_expert_hidden * expert_pre[:, :, 1] * expert_slope, grad_expert_hidden * expert_act],
        axis=2,
    ).astype(jnp.bfloat16)
    outer_expert = jnp.einsum(
        "erf,erd->efd", expert_hidden, grad_rows_in, preferred_element_type=jnp.float32
    )
    inner_expert = jnp.einsum(
        "erd,ergf->edgf", expert_rows, grad_expert_pre, preferred_element_type=jnp.float32
    )
    grad_rows_out = jnp.einsum(
        "ergf,edgf->erd", grad_expert_pre, expert_inner, preferred_element_type=jnp.float32
    )
    returned_back = (
        lax.all_to_all(
            grad_rows_out[None].astype(jnp.bfloat16),
            ("fsdp", "ctx"),
            split_axis=2,
            concat_axis=0,
            tiled=True,
        )
        .astype(jnp.float32)
        .reshape(experts * capacity, width)
    )
    for route_slot in range(TOP):
        grad_normed_part = (
            grad_normed_part
            + keep_weight[:, route_slot][:, None] * returned_back[pair_index[:, route_slot]]
        )
    grad_normed_sum, shared_total, gate_total = lax.psum(
        (grad_normed_part, shared_dot, gate_dot), "tp"
    )
    grad_blend = (blend * (1.0 - blend) * shared_total).astype(jnp.bfloat16)
    grad_gate = keep_weight * gate_total
    grad_probs = jnp.sum(onehot * grad_gate[:, :, None], axis=1)
    grad_logits = (
        router_probs * (grad_probs - jnp.sum(router_probs * grad_probs, axis=-1, keepdims=True))
    ).astype(jnp.bfloat16)
    router_grad_part = jnp.einsum(
        "td,te->de", second_normalized, grad_logits, preferred_element_type=jnp.float32
    )
    blend_grad_part = jnp.einsum(
        "td,t->d", second_normalized, grad_blend, preferred_element_type=jnp.float32
    )
    grad_normed_two = (
        grad_normed_sum
        + jnp.einsum("te,de->td", grad_logits, router_weight, preferred_element_type=jnp.float32)
        + grad_blend.astype(jnp.float32)[:, None] * blend_weight.astype(jnp.float32)[None, :]
    )
    after_norm_grad, gain_two_grad = jax.vjp(root_norm, after_attn, gains[1])[1](grad_normed_two)
    grad_after = grad_y + after_norm_grad
    grad_attn = grad_after.astype(jnp.bfloat16)
    projection_full = jnp.einsum(
        "tm,td->md", mixed_result, grad_attn, preferred_element_type=jnp.float32
    )
    grad_mixed = (
        jnp.einsum("td,md->tm", grad_attn, out_full, preferred_element_type=jnp.float32)
        .astype(jnp.bfloat16)
        .reshape(seq_count, half_len, local_heads, HEAD_DIM)
    )
    sequence = 0
    grad_query, grad_key, grad_value = attend_backward(
        queries[sequence],
        keys_all[sequence],
        values_all[sequence],
        allowed[sequence],
        log_parts[sequence],
        grad_mixed[sequence],
        score_scale,
    )
    query_parts = [grad_query]
    key_parts = [grad_key]
    value_parts = [grad_value]
    grad_queries = jnp.stack(query_parts)
    grad_keys = jnp.stack(key_parts)
    grad_values = jnp.stack(value_parts)
    sent_keys, sent_values = (
        from_behind(grad_keys[:, :half_len].astype(jnp.bfloat16), "ctx", -1).astype(jnp.float32),
        from_behind(grad_values[:, :half_len].astype(jnp.bfloat16), "ctx", -1).astype(jnp.float32),
    )
    grad_keys_own = grad_keys[:, half_len:] + sent_keys
    grad_values_own = grad_values[:, half_len:] + sent_values
    grad_linear = (
        jnp.stack(
            [
                rotate_back(grad_queries, cosine, sine_table),
                rotate_back(grad_keys_own, cosine, sine_table),
                grad_values_own,
            ],
            axis=2,
        )
        .astype(jnp.bfloat16)
        .reshape(tokens, 3, local_width)
    )
    bias_part = jnp.sum(grad_linear.astype(jnp.float32), axis=0)
    qkv_grad_full = jnp.einsum(
        "td,tcm->dcm", first_normalized, grad_linear, preferred_element_type=jnp.float32
    )
    grad_normed_one = lax.psum(
        jnp.einsum("tcm,dcm->td", grad_linear, qkv_full, preferred_element_type=jnp.float32).astype(
            jnp.bfloat16
        ),
        "tp",
    ).astype(jnp.float32)
    residual_norm_grad, gain_one_grad = jax.vjp(root_norm, residual, gains[0])[1](grad_normed_one)
    input_grad = (
        (grad_after + residual_norm_grad).astype(jnp.bfloat16).reshape(seq_count, half_len, width)
    )
    qkv_grad, projection_grad, inner_shared, outer_shared = (
        lax.psum_scatter(
            qkv_grad_full.astype(jnp.bfloat16), ("fsdp", "ctx"), scatter_dimension=0, tiled=True
        ).astype(jnp.float32),
        lax.psum_scatter(
            projection_full.astype(jnp.bfloat16), ("fsdp", "ctx"), scatter_dimension=1, tiled=True
        ).astype(jnp.float32),
        lax.psum_scatter(
            inner_grad_full.astype(jnp.bfloat16), ("fsdp", "ctx"), scatter_dimension=0, tiled=True
        ).astype(jnp.float32),
        lax.psum_scatter(
            outer_grad_full.astype(jnp.bfloat16), ("fsdp", "ctx"), scatter_dimension=1, tiled=True
        ).astype(jnp.float32),
    )
    gains_grad, bias_grad, router_grad, blend_grad = (
        lax.psum(
            jnp.stack([gain_one_grad, gain_two_grad]).astype(jnp.bfloat16), ("fsdp", "ctx")
        ).astype(jnp.float32),
        lax.psum(bias_part.astype(jnp.bfloat16), ("fsdp", "ctx")).astype(jnp.float32),
        lax.psum(router_grad_part.astype(jnp.bfloat16), ("fsdp", "ctx")).astype(jnp.float32),
        lax.psum(blend_grad_part.astype(jnp.bfloat16), ("fsdp", "ctx")).astype(jnp.float32),
    )
    return (
        layer_out,
        input_grad,
        gains_grad,
        qkv_grad,
        bias_grad,
        projection_grad,
        router_grad,
        blend_grad,
        inner_shared,
        outer_shared,
        inner_expert,
        outer_expert,
    )


VMEM = pl.BlockSpec(memory_space=pltpu.VMEM)
SMEM = pl.BlockSpec(memory_space=pltpu.SMEM)
ANY = pl.BlockSpec(memory_space=pl.ANY)
ROWS_COLS = (((1,), (0,)), ((), ()))
ROWS_ROWS = (((1,), (1,)), ((), ()))
COLS_COLS = (((0,), (0,)), ((), ()))


def product(one, other, dims=ROWS_COLS):
    return lax.dot_general(one, other, dims, preferred_element_type=jnp.float32)


def call(kernel, shapes, flops, moved, room=40, **others):
    return pl.pallas_call(
        kernel,
        out_shape=shapes,
        compiler_params=pltpu.CompilerParams(vmem_limit_bytes=room * 2**20),
        cost_estimate=pl.CostEstimate(
            flops=int(flops), bytes_accessed=int(moved), transcendentals=0
        ),
        **others,
    )


def after(values, *earlier):
    return lax.optimization_barrier((values, earlier))[0]


def swap_x(values):
    return lax.ppermute(values, "fsdp", [(f, f ^ 2) for f in range(4)])


def swap_core(values):
    return lax.ppermute(values, "fsdp", [(f, f ^ 1) for f in range(4)])


def swap_y(values):
    return lax.ppermute(values, "ctx", [(0, 1), (1, 0)])


def own_number():
    return lax.axis_index("fsdp") * 2 + lax.axis_index("ctx")


def exchange_order(parts):
    number = own_number()
    for bit in (4, 2, 1):
        taken = (number & bit) != 0
        parts = [jnp.where(taken, parts[i ^ bit], parts[i]) for i in range(8)]
    return parts


def add_low(one, other):
    return (one.astype(jnp.float32) + other.astype(jnp.float32)).astype(jnp.bfloat16)


def halves_sum(own, arrived):
    half = own.shape[0] // 2
    return add_low(own[:half], arrived[:half]), add_low(own[half:], arrived[half:])


def first_hops(taken):
    return swap_x(taken[1][0]), swap_y(taken[2][1]), swap_x(taken[3][0]), swap_y(taken[3][1])


def last_parts(taken, hops):
    _, _, both_low, both_high = hops
    return add_low(taken[1][1], both_high), add_low(taken[2][0], both_low)


def last_hops(parts):
    return swap_x(parts[0]), swap_y(parts[1])


def hops_sum(taken, hops, ends):
    x_low, y_high, _, _ = hops
    x_high, y_low = ends
    sums = [
        mine.astype(jnp.float32) + along_x.astype(jnp.float32) + along_y.astype(jnp.float32)
        for mine, along_x, along_y in ((taken[0][0], x_low, y_low), (taken[0][1], x_high, y_high))
    ]
    return jnp.concatenate(sums).astype(jnp.bfloat16)


def sum_eight(values):
    values = values + swap_core(values)
    values = values + swap_x(values)
    return values + swap_y(values)


def sum_line(values):
    count = lax.axis_size("tp")
    bit = 1
    while bit < count:
        values = values + lax.ppermute(values, "tp", [(i, i ^ bit) for i in range(count)])
        bit *= 2
    return values


def line_reduce(rows):
    count = lax.axis_size("tp")
    blocks = rows.reshape((count, rows.shape[0] // count) + rows.shape[1:])
    arrived = lax.all_to_all(blocks, "tp", split_axis=0, concat_axis=0, tiled=True)
    return jnp.sum(arrived.astype(jnp.float32), axis=0)


def line_gather(block):
    copies = jnp.broadcast_to(block[None], (lax.axis_size("tp"),) + block.shape)
    return lax.all_to_all(copies, "tp", split_axis=0, concat_axis=0, tiled=True)


def pick(blocks, index):
    return lax.dynamic_index_in_dim(blocks, index, axis=0, keepdims=False)


def hop_reduce(rows, earlier=()):
    count = lax.axis_size("tp")
    me = lax.axis_index("tp")
    blocks = rows.reshape((count, rows.shape[0] // count) + rows.shape[1:])
    right, left, first = None, None, None
    for step in range(1, count):
        if step == 2:
            right, left = first = after((right, left), earlier)
        to_right = pick(blocks, jnp.minimum(count - step + me, count - 1))
        to_left = pick(blocks, jnp.maximum(step + me - count, 0))
        if step > 1:
            to_right, to_left = add_low(to_right, right), add_low(to_left, left)
        right = lax.ppermute(to_right, "tp", [(i, i + 1) for i in range(min(step, count - 1))])
        left = lax.ppermute(
            to_left, "tp", [(i, i - 1) for i in range(max(count - step, 1), count)]
        )
    total = (
        pick(blocks, me).astype(jnp.float32)
        + right.astype(jnp.float32)
        + left.astype(jnp.float32)
    )
    return total, first


def hop_gather(block):
    count = lax.axis_size("tp")
    me = lax.axis_index("tp")
    right, left = [block], [block]
    for step in range(1, count):
        right.append(
            lax.ppermute(right[-1], "tp", [(i, i + 1) for i in range(step - 1, count - 1)])
        )
        left.append(
            lax.ppermute(left[-1], "tp", [(i, i - 1) for i in range(1, count - step + 1)])
        )
    result = []
    for place in range(count):
        taken = block
        for step in range(1, count):
            taken = jnp.where(place == me - step, right[step], taken)
            taken = jnp.where(place == me + step, left[step], taken)
        result.append(taken)
    return jnp.concatenate(result)


def trade_chips(parts):
    return (
        swap_y(jnp.concatenate([parts[1], parts[3]])),
        swap_x(jnp.concatenate([parts[4], parts[6]])),
        lax.ppermute(
            jnp.concatenate([parts[5], parts[7]]),
            ("fsdp", "ctx"),
            [(d, d ^ 5) for d in range(8)],
        ),
    )


def trade_cores(parts, arrived):
    rows = parts[0].shape[0]
    from_y, from_x, both = arrived
    sibling = swap_core(
        jnp.concatenate([parts[2], from_y[rows:], from_x[rows:], both[rows:]])
    )
    return [
        parts[0],
        from_y[:rows],
        sibling[:rows],
        sibling[rows : 2 * rows],
        from_x[:rows],
        both[:rows],
        sibling[2 * rows : 3 * rows],
        sibling[3 * rows :],
    ]


def columns_of(values, count):
    wide = values.shape[1] // count
    return [values[:, i * wide : (i + 1) * wide] for i in range(count)]


def block_columns(index, wide):
    return pl.ds(pl.multiple_of(index * wide, wide), wide)


def turn(values, cosine, signed_sine):
    return values * cosine + pltpu.roll(values, HEAD_DIM // 2, 1) * signed_sine


def pieces_of(lists):
    flat, places = [], []
    for pieces in lists:
        places.append(range(len(flat), len(flat) + len(pieces)))
        flat += pieces
    return flat, places


def project(number, hidden, gain, weights, bias, cosine, signed_sine):
    tokens, width = hidden.shape
    local_width = bias.shape[2]
    deep = width // 8

    flat, places = pieces_of(weights)

    def kernel(number_ref, hidden_ref, gain_ref, bias_ref, cos_ref, sin_ref, *others):
        weight_refs, (out_ref, normed_ref) = others[: len(flat)], others[len(flat) :]
        part = pl.program_id(0)

        @pl.when(part == 0)
        def _():
            values = hidden_ref[...].astype(jnp.float32)
            normed_ref[...] = root_norm(values, gain_ref[...]).astype(jnp.bfloat16)

        total = None
        for r in range(8):
            rows = normed_ref[:, block_columns(number_ref[0] ^ r, deep)]
            terms = [product(rows, weight_refs[at][0]) for at in places[r]]
            term = terms[0] if len(terms) == 1 else jnp.concatenate(terms, axis=1)
            total = term if total is None else total + term
        total = total + bias_ref[0]
        cosine_now = jnp.where(part < 2, cos_ref[...], 1.0)
        sine_now = jnp.where(part < 2, sin_ref[...], 0.0)
        for h in range(local_width // HEAD_DIM):
            at = slice(h * HEAD_DIM, (h + 1) * HEAD_DIM)
            out_ref[0, :, at] = turn(total[:, at], cosine_now, sine_now).astype(jnp.bfloat16)

    whole = lambda *shape: pl.BlockSpec(shape, lambda c: (0,) * len(shape))
    return call(
        kernel,
        [
            jax.ShapeDtypeStruct((3, tokens, local_width), jnp.bfloat16),
            jax.ShapeDtypeStruct((tokens, width), jnp.bfloat16),
        ],
        2 * tokens * width * 3 * local_width,
        2 * (2 * tokens * width + 3 * width * local_width + 3 * tokens * local_width),
        grid=(3,),
        in_specs=[
            SMEM,
            whole(tokens, width),
            whole(1, width),
            pl.BlockSpec((1, 1, local_width), lambda c: (c, 0, 0)),
            whole(tokens, HEAD_DIM),
            whole(tokens, HEAD_DIM),
        ]
        + [pl.BlockSpec((1,) + piece.shape[1:], lambda c: (c, 0, 0)) for piece in flat],
        out_specs=[
            pl.BlockSpec((1, tokens, local_width), lambda c: (c, 0, 0)),
            whole(tokens, width),
        ],
    )(number, hidden, gain, bias, cosine, signed_sine, *flat)


ATTEND_ROWS = 176


def attend(projected, prior, masks, score_scale):
    _, tokens, local_width = projected.shape
    heads = local_width // HEAD_DIM
    tiles = tokens // ATTEND_ROWS

    def kernel(q_ref, own_ref, prior_ref, mask_own_ref, mask_prior_ref, mixed_ref, log_ref):
        for h in range(heads):
            at = slice(h * HEAD_DIM, (h + 1) * HEAD_DIM)
            queries = q_ref[0, :, at]
            score_own = product(queries, own_ref[1, :, at], ROWS_ROWS) * score_scale
            score_own = score_own + mask_own_ref[...]
            score_prior = product(queries, prior_ref[0, :, at], ROWS_ROWS) * score_scale
            score_prior = score_prior + mask_prior_ref[...]
            row_max = jnp.maximum(
                jnp.max(score_own, axis=-1, keepdims=True),
                jnp.max(score_prior, axis=-1, keepdims=True),
            )
            own = jnp.exp(score_own - row_max)
            before = jnp.exp(score_prior - row_max)
            total = jnp.sum(own, axis=-1, keepdims=True) + jnp.sum(before, axis=-1, keepdims=True)
            scale = 1.0 / total
            mixed = product((own * scale).astype(jnp.bfloat16), own_ref[2, :, at])
            mixed = mixed + product((before * scale).astype(jnp.bfloat16), prior_ref[1, :, at])
            mixed_ref[:, at] = mixed.astype(jnp.bfloat16)
            log_ref[:, h : h + 1] = row_max + jnp.log(total)

    return call(
        kernel,
        [
            jax.ShapeDtypeStruct((tokens, local_width), jnp.bfloat16),
            jax.ShapeDtypeStruct((tokens, heads), jnp.float32),
        ],
        8 * tokens * tokens * local_width,
        8 * tokens * tokens + 12 * tokens * local_width,
        grid=(tiles,),
        in_specs=[
            pl.BlockSpec((1, ATTEND_ROWS, local_width), lambda i: (0, i, 0)),
            pl.BlockSpec((3, tokens, local_width), lambda i: (0, 0, 0)),
            pl.BlockSpec((2, tokens, local_width), lambda i: (0, 0, 0)),
            pl.BlockSpec((ATTEND_ROWS, tokens), lambda i: (i, 0)),
            pl.BlockSpec((ATTEND_ROWS, tokens), lambda i: (i, 0)),
        ],
        out_specs=[
            pl.BlockSpec((ATTEND_ROWS, local_width), lambda i: (i, 0)),
            pl.BlockSpec((ATTEND_ROWS, heads), lambda i: (i, 0)),
        ],
    )(projected, projected, prior, *masks)


def attend_back(projected, prior, masks, log_total, grad_mixed, cosine, signed_sine, score_scale):
    _, tokens, local_width = projected.shape
    heads = local_width // HEAD_DIM
    tiles = tokens // ATTEND_ROWS

    def kernel(
        q_ref, own_ref, prior_ref, mask_own_ref, mask_prior_ref, log_ref, grad_ref, cos_ref, sin_ref,
        query_out, own_out, prior_out, own_sum, prior_sum,
    ):
        tile = pl.program_id(0)

        @pl.when(tile == 0)
        def _():
            own_sum[...] = jnp.zeros_like(own_sum)
            prior_sum[...] = jnp.zeros_like(prior_sum)

        for h in range(heads):
            at = slice(h * HEAD_DIM, (h + 1) * HEAD_DIM)
            queries = q_ref[0, :, at]
            grads = grad_ref[:, at]
            log_now = log_ref[:, h : h + 1]
            soft, low, dots = [], [], []
            for keys, values, mask_ref in (
                (own_ref[1, :, at], own_ref[2, :, at], mask_own_ref),
                (prior_ref[0, :, at], prior_ref[1, :, at], mask_prior_ref),
            ):
                score = product(queries, keys, ROWS_ROWS) * score_scale + mask_ref[...]
                soft.append(jnp.exp(score - log_now))
                dots.append(product(grads, values, ROWS_ROWS))
            centre = jnp.sum(soft[0] * dots[0], axis=-1, keepdims=True)
            centre = centre + jnp.sum(soft[1] * dots[1], axis=-1, keepdims=True)
            grad_query = None
            for side, sums, keys in (
                (0, own_sum, own_ref[1, :, at]),
                (1, prior_sum, prior_ref[0, :, at]),
            ):
                grad_score = (soft[side] * (dots[side] - centre)).astype(jnp.bfloat16)
                term = product(grad_score, keys)
                grad_query = term if grad_query is None else grad_query + term
                sums[0, :, at] += product(grad_score, queries, COLS_COLS)
                sums[1, :, at] += product(soft[side].astype(jnp.bfloat16), grads, COLS_COLS)
            query_out[:, at] = turn(
                grad_query * score_scale, cos_ref[...], -sin_ref[...]
            ).astype(jnp.bfloat16)

        @pl.when(tile == tiles - 1)
        def _():
            own_out[0] = own_sum[0] * score_scale
            own_out[1] = own_sum[1]
            prior_out[0] = (prior_sum[0] * score_scale).astype(jnp.bfloat16)
            prior_out[1] = prior_sum[1].astype(jnp.bfloat16)

    row_block = lambda wide: pl.BlockSpec((ATTEND_ROWS, wide), lambda i: (i, 0))
    whole = lambda *shape: pl.BlockSpec(shape, lambda i: (0,) * len(shape))
    pair = (2, tokens, local_width)
    return call(
        kernel,
        [
            jax.ShapeDtypeStruct((tokens, local_width), jnp.bfloat16),
            jax.ShapeDtypeStruct(pair, jnp.float32),
            jax.ShapeDtypeStruct(pair, jnp.bfloat16),
        ],
        20 * tokens * tokens * local_width,
        8 * tokens * tokens + 30 * tokens * local_width,
        grid=(tiles,),
        in_specs=[
            pl.BlockSpec((1, ATTEND_ROWS, local_width), lambda i: (0, i, 0)),
            whole(3, tokens, local_width),
            whole(2, tokens, local_width),
            row_block(tokens),
            row_block(tokens),
            row_block(heads),
            row_block(local_width),
            row_block(HEAD_DIM),
            row_block(HEAD_DIM),
        ],
        out_specs=[row_block(local_width), whole(*pair), whole(*pair)],
        scratch_shapes=[pltpu.VMEM(pair, jnp.float32), pltpu.VMEM(pair, jnp.float32)],
    )(projected, projected, prior, *masks, log_total, grad_mixed, cosine, signed_sine)


def project_back(number, grad_query, grad_own, arrived, cosine, signed_sine, hidden, weights):
    tokens, local_width = grad_query.shape
    flat, places = pieces_of(weights)
    deep = flat[0].shape[1]
    width = 8 * deep
    rows = tokens // 2

    def kernel(number_ref, query_ref, own_ref, arrived_ref, cos_ref, sin_ref, hidden_ref, *others):
        weight_refs = others[: len(flat)]
        linear_ref, bias_ref, gain_ref, out_ref = others[len(flat) :]

        @pl.when(pl.program_id(0) == 0)
        def _():
            bias_ref[...] = jnp.zeros_like(bias_ref)
            gain_ref[...] = jnp.zeros_like(gain_ref)

        residual = hidden_ref[...].astype(jnp.float32)
        scale = lax.rsqrt(jnp.mean(residual * residual, axis=-1, keepdims=True) + norm_epsilon)

        keys = own_ref[0] + arrived_ref[0].astype(jnp.float32)
        linear_ref[0] = query_ref[...]
        for h in range(local_width // HEAD_DIM):
            at = slice(h * HEAD_DIM, (h + 1) * HEAD_DIM)
            linear_ref[1, :, at] = turn(keys[:, at], cos_ref[...], -sin_ref[...]).astype(
                jnp.bfloat16
            )
        linear_ref[2] = (own_ref[1] + arrived_ref[1].astype(jnp.float32)).astype(jnp.bfloat16)
        for c in range(3):
            bias_ref[c] += jnp.sum(linear_ref[c].astype(jnp.float32), axis=0, keepdims=True)
        for r in range(8):
            total = None
            for c in range(3):
                first = 0
                for at in places[r]:
                    last = first + flat[at].shape[2]
                    term = product(linear_ref[c, :, first:last], weight_refs[at][c], ROWS_ROWS)
                    total = term if total is None else total + term
                    first = last
            columns = block_columns(number_ref[0] ^ r, deep)
            out_ref[:, columns] = total.astype(jnp.bfloat16)
            scaled = hidden_ref[:, columns].astype(jnp.float32) * scale
            gain_ref[:, columns] += jnp.sum(total * scaled, axis=0, keepdims=True)

    whole = lambda *shape: pl.BlockSpec(shape, lambda i: (0,) * len(shape))
    row_block = lambda wide: pl.BlockSpec((rows, wide), lambda i: (i, 0))
    pair_block = pl.BlockSpec((2, rows, local_width), lambda i: (0, i, 0))
    return call(
        kernel,
        [
            jax.ShapeDtypeStruct((3, tokens, local_width), jnp.bfloat16),
            jax.ShapeDtypeStruct((3, 1, local_width), jnp.float32),
            jax.ShapeDtypeStruct((1, width), jnp.float32),
            jax.ShapeDtypeStruct((tokens, width), jnp.bfloat16),
        ],
        6 * tokens * local_width * width,
        2 * (tokens * width + 3 * width * local_width + 12 * tokens * local_width),
        grid=(2,),
        in_specs=[
            SMEM,
            row_block(local_width),
            pair_block,
            pair_block,
            row_block(HEAD_DIM),
            row_block(HEAD_DIM),
            row_block(width),
        ]
        + [whole(*piece.shape) for piece in flat],
        out_specs=[
            pl.BlockSpec((3, rows, local_width), lambda i: (0, i, 0)),
            whole(3, 1, local_width),
            whole(1, width),
            row_block(width),
        ],
    )(number, grad_query, grad_own, arrived, cosine, signed_sine, hidden, *flat)


def project_weights(normed, grad_linear):
    tokens, width = normed.shape
    local_width = grad_linear.shape[2]
    deep = width // 8

    def kernel(normed_ref, linear_ref, out_ref):
        columns = block_columns(pl.program_id(0), deep)
        for c in range(3):
            out_ref[0, c] = product(normed_ref[:, columns], linear_ref[c], COLS_COLS).astype(
                jnp.bfloat16
            )

    whole = lambda *shape: pl.BlockSpec(shape, lambda i: (0,) * len(shape))
    return call(
        kernel,
        jax.ShapeDtypeStruct((8, 3, deep, local_width), jnp.bfloat16),
        6 * tokens * local_width * width,
        2 * (tokens * width + 3 * width * local_width + 3 * tokens * local_width),
        grid=(8,),
        in_specs=[whole(tokens, width), whole(3, tokens, local_width)],
        out_specs=pl.BlockSpec((1, 3, deep, local_width), lambda i: (i, 0, 0, 0)),
    )(normed, grad_linear)


def lay_weights(expert_t, expert_outer, shared_rows, router_rows, pad):
    _, hid_e, width = expert_t.shape
    hid_s = shared_rows.shape[0] // 3
    hid = hid_e + hid_s
    last = hid + router_rows.shape[0]

    def kernel(expert_ref, outer_ref, shared_ref, router_ref, inner_out, outer_out):
        zeros = jnp.zeros((pad - hid, width), jnp.bfloat16)
        inner_out[:hid_e] = expert_ref[0]
        inner_out[hid_e:hid] = shared_ref[:hid_s]
        inner_out[hid:last] = router_ref[...]
        inner_out[last:pad] = zeros[: pad - last]
        inner_out[pad : pad + hid_e] = expert_ref[1]
        inner_out[pad + hid_e : pad + hid] = shared_ref[hid_s : 2 * hid_s]
        inner_out[pad + hid :] = zeros
        outer_out[:hid_e] = outer_ref[...]
        outer_out[hid_e:hid] = shared_ref[2 * hid_s :]
        outer_out[hid:] = zeros

    return call(
        kernel,
        [
            jax.ShapeDtypeStruct((2 * pad, width), jnp.bfloat16),
            jax.ShapeDtypeStruct((pad, width), jnp.bfloat16),
        ],
        0,
        12 * pad * width,
        in_specs=[VMEM] * 4,
        out_specs=[VMEM] * 2,
    )(expert_t, expert_outer, shared_rows, router_rows)


MIX_ROWS = 352
LANES = 128


def tiles_of(pieces):
    return [(at, first) for at, p in enumerate(pieces) for first in range(0, p.shape[0], MIX_ROWS)]


def next_tile(refs, starts, buffer, sems):
    tile = pl.program_id(0)

    def copy(number):
        at, first = starts[number]
        return pltpu.make_async_copy(
            refs[at].at[pl.ds(first, MIX_ROWS)], buffer.at[number % 2], sems.at[number % 2]
        )

    for number in range(len(starts)):

        @pl.when(tile == number)
        def _():
            if number == 0:
                copy(0).start()
            if number + 1 < len(starts):
                copy(number + 1).start()
            copy(number).wait()

    return buffer[lax.rem(tile, 2)]


CHIPS = (2, 0, 6, 4, 3, 1, 7, 5)


def narrow(numbers, blocks, chosen, other):
    gathered = not isinstance(blocks, list)
    blocks = [blocks] if gathered else blocks
    each, width = blocks[0].shape[-2:]
    units = other.shape[0]
    tiles = each // MIX_ROWS
    starts = [(at, t * MIX_ROWS) for at in range(len(chosen)) for t in range(tiles)]

    def kernel(numbers_ref, other_ref, *refs):
        block_refs, (out_ref, buffer, sems) = refs[: len(blocks)], refs[len(blocks) :]
        tile = pl.program_id(0)

        def copy(number):
            at, first = starts[number]
            block = block_refs[0].at[numbers_ref[0] ^ chosen[at]] if gathered else block_refs[at]
            return pltpu.make_async_copy(
                block.at[pl.ds(first, MIX_ROWS)],
                buffer.at[number % 2],
                sems.at[number % 2],
            )

        for number in range(len(starts)):

            @pl.when(tile == number)
            def _():
                if number == 0:
                    copy(0).start()
                if number + 1 < len(starts):
                    copy(number + 1).start()
                copy(number).wait()

        out_ref[...] = product(buffer[lax.rem(tile, 2)], other_ref[...], ROWS_ROWS)

    tokens = len(starts) * MIX_ROWS
    return call(
        kernel,
        jax.ShapeDtypeStruct((tokens, units), jnp.float32),
        2 * tokens * units * width,
        2 * (tokens * width + units * width + 2 * tokens * units),
        grid=(len(starts),),
        in_specs=[SMEM, pl.BlockSpec((units, width), lambda i: (0, 0))] + [ANY] * len(blocks),
        out_specs=pl.BlockSpec((MIX_ROWS, units), lambda i: (i, 0)),
        scratch_shapes=[
            pltpu.VMEM((2, MIX_ROWS, width), jnp.bfloat16),
            pltpu.SemaphoreType.DMA((2,)),
        ],
    )(numbers, other, *blocks)


def widen(parts, other):
    starts = tiles_of(parts)
    units, width = other.shape
    rows = parts[0].shape[0] // 2
    each = rows // MIX_ROWS
    count = 2 * len(parts)

    def kernel(other_ref, *refs):
        part_refs = refs[: len(parts)]
        outs, (buffer, sems) = refs[len(parts) : len(parts) + count], refs[len(parts) + count :]
        value = product(next_tile(part_refs, starts, buffer, sems), other_ref[...])
        for at in range(count):

            @pl.when(pl.program_id(0) // each == at)
            def _():
                outs[at][...] = value.astype(jnp.bfloat16)

    def place(at):
        return pl.BlockSpec(
            (MIX_ROWS, width), lambda i: (jnp.clip(i - at * each, 0, each - 1), 0)
        )

    tokens = count * rows
    return call(
        kernel,
        [jax.ShapeDtypeStruct((rows, width), jnp.bfloat16)] * count,
        2 * tokens * units * width,
        2 * (tokens * width + units * width + tokens * units),
        grid=(len(starts),),
        in_specs=[pl.BlockSpec((units, width), lambda i: (0, 0))] + [ANY] * len(parts),
        out_specs=[place(at) for at in range(count)],
        scratch_shapes=[
            pltpu.VMEM((2, MIX_ROWS, units), jnp.bfloat16),
            pltpu.SemaphoreType.DMA((2,)),
        ],
    )(other, *parts)


def mixture(row_pieces, upstream, chip, kept, mine, inner, hid_e, hid, experts):
    tokens, pad = kept.shape[0], upstream.shape[1]
    width = inner.shape[1]
    starts = tiles_of(row_pieces)
    tiles = len(starts)
    count = len(row_pieces)
    first_router = hid - (pad - LANES)

    def kernel(kept_ref, mine_ref, inner_ref, upstream_ref, *others):
        row_refs = others[:count]
        pre_out, weighted_out, other_out, own_out, buffer, sems = others[count:]
        tile = pl.program_id(0)
        rows = next_tile(row_refs, starts, buffer, sems)
        pre = product(rows, inner_ref[...], ROWS_ROWS)
        upstream = upstream_ref[...]
        gate_pre, up_pre = pre[:, :pad], pre[:, pad:]
        tail = gate_pre[:, pad - LANES :]
        lane = lax.broadcasted_iota(jnp.int32, tail.shape, 1) - first_router
        routed = (lane >= 0) & (lane < experts)
        logits = jnp.where(routed, tail, -1e30)
        raised = jnp.exp(logits - jnp.max(logits, axis=-1, keepdims=True))
        probs = raised / jnp.sum(raised, axis=-1, keepdims=True)
        own_prob = jnp.sum(probs * mine_ref[...], axis=-1, keepdims=True)
        blend = jax.nn.sigmoid(
            jnp.sum(jnp.where(lane == experts, tail, 0.0), axis=-1, keepdims=True)
        )
        kept_now = kept_ref[...]
        of_expert = lax.broadcasted_iota(jnp.int32, gate_pre.shape, 1) < hid_e
        weight = jnp.where(of_expert, kept_now * own_prob, blend)
        sigma = jax.nn.sigmoid(gate_pre)
        act = gate_pre * sigma
        slope = sigma + act * (1.0 - sigma)
        hidden = (act * up_pre).astype(jnp.bfloat16).astype(jnp.float32)
        inner_dot = hidden * upstream
        gate_dot = jnp.sum(jnp.where(of_expert, inner_dot, 0.0), axis=-1, keepdims=True)
        blend_dot = jnp.sum(jnp.where(of_expert, 0.0, inner_dot), axis=-1, keepdims=True)
        grad_router = probs * (kept_now * gate_dot) * (mine_ref[...] - own_prob)
        grad_blend = blend * (1.0 - blend) * blend_dot
        scaled = weight * upstream
        grad_gate = scaled * up_pre * slope
        grad_tail = grad_gate[:, pad - LANES :] + jnp.where(
            lane == experts, grad_blend, grad_router
        )
        pre_out[:, : pad - LANES] = grad_gate[:, : pad - LANES].astype(jnp.bfloat16)
        pre_out[:, pad - LANES : pad] = grad_tail.astype(jnp.bfloat16)
        pre_out[:, pad:] = (scaled * act).astype(jnp.bfloat16)
        weighted_out[...] = (weight * hidden).astype(jnp.bfloat16)
        back = product(pre_out[...], inner_ref[...]).astype(jnp.bfloat16)

        @pl.when(tile < tiles // 2)
        def _():
            other_out[...] = back

        @pl.when(tile >= tiles // 2)
        def _():
            own_out[...] = back

    whole = lambda *shape: pl.BlockSpec(shape, lambda i: (0,) * len(shape))
    row_block = lambda wide: pl.BlockSpec((MIX_ROWS, wide), lambda i: (i, 0))
    half = jax.ShapeDtypeStruct((tokens // 2, width), jnp.bfloat16)
    return call(
        kernel,
        [
            jax.ShapeDtypeStruct((tokens, 2 * pad), jnp.bfloat16),
            jax.ShapeDtypeStruct((tokens, pad), jnp.bfloat16),
            half,
            half,
        ],
        8 * tokens * pad * width,
        2 * (2 * tokens * width + 5 * tokens * pad + 2 * pad * width),
        grid=(tiles,),
        in_specs=[
            row_block(1),
            whole(1, LANES),
            whole(2 * pad, width),
            pl.BlockSpec((MIX_ROWS, pad), lambda i: (i + chip * tiles, 0)),
        ]
        + [ANY] * count,
        out_specs=[
            row_block(2 * pad),
            row_block(pad),
            pl.BlockSpec((MIX_ROWS, width), lambda i: (jnp.minimum(i, tiles // 2 - 1), 0)),
            pl.BlockSpec((MIX_ROWS, width), lambda i: (jnp.maximum(i - tiles // 2, 0), 0)),
        ],
        scratch_shapes=[
            pltpu.VMEM((2, MIX_ROWS, width), jnp.bfloat16),
            pltpu.SemaphoreType.DMA((2,)),
        ],
    )(kept, mine, inner, upstream, *row_pieces)


def attend_out(numbers, hidden, gain, mixed, own_weights, other_weights):
    tokens, width = hidden.shape
    count, _, local_width = mixed.shape
    deep = own_weights[0].shape[1]
    long = count * local_width
    rows = tokens // count

    def kernel(numbers_ref, hidden_ref, gain_ref, mixed_ref, *others):
        own_refs, (other_ref, normed_ref, kept_ref, sum_ref) = others[:4], others[4:]
        heads = jnp.concatenate([mixed_ref[i] for i in range(count)], axis=1)
        for r in range(8):
            chip = (r // 4) * 2 + r % 2
            if (r // 2) % 2:
                weight = other_ref[chip * long : (chip + 1) * long]
            else:
                weight = own_refs[chip][...]
            columns = block_columns(numbers_ref[0] ^ r, deep)
            sum_ref[:, columns] = hidden_ref[:, columns].astype(jnp.float32) + product(
                heads, weight
            )
        values = sum_ref[...]
        normed_ref[...] = root_norm(values, gain_ref[...]).astype(jnp.bfloat16)

        @pl.when(pl.program_id(0) == numbers_ref[1])
        def _():
            kept_ref[...] = values

    whole = lambda *shape: pl.BlockSpec(shape, lambda i: (0,) * len(shape))
    row_block = lambda wide: pl.BlockSpec((rows, wide), lambda i: (i, 0))
    return call(
        kernel,
        [
            jax.ShapeDtypeStruct((tokens, width), jnp.bfloat16),
            jax.ShapeDtypeStruct((rows, width), jnp.float32),
        ],
        2 * tokens * width * long,
        2 * (3 * tokens * width + long * width),
        room=62,
        grid=(count,),
        in_specs=[
            SMEM,
            row_block(width),
            whole(1, width),
            pl.BlockSpec((count, rows, local_width), lambda i: (0, i, 0)),
        ]
        + [whole(long, deep)] * 4
        + [whole(4 * long, deep)],
        out_specs=[row_block(width), whole(rows, width)],
        scratch_shapes=[pltpu.VMEM((rows, width), jnp.float32)],
    )(numbers, hidden, gain, mixed, *own_weights, other_weights)


def attend_out_back(numbers, grads, own_weights, other_weights, count):
    rows, width = grads.shape
    long, deep = own_weights[0].shape
    local_width = long // count

    def kernel(numbers_ref, grads_ref, *others):
        own_refs, (other_ref, mixed_ref) = others[:4], others[4:]
        for i in range(count):
            total = None
            for r in range(8):
                chip = (r // 4) * 2 + r % 2
                first = i * local_width
                if (r // 2) % 2:
                    weight = other_ref[chip * long + first : chip * long + first + local_width]
                else:
                    weight = own_refs[chip][first : first + local_width]
                taken = grads_ref[:, block_columns(numbers_ref[0] ^ r, deep)]
                term = product(taken, weight, ROWS_ROWS)
                total = term if total is None else total + term
            mixed_ref[i] = total.astype(jnp.bfloat16)

    whole = lambda *shape: pl.BlockSpec(shape, lambda i: (0,) * len(shape))
    return call(
        kernel,
        jax.ShapeDtypeStruct((count, rows, local_width), jnp.bfloat16),
        2 * rows * width * long,
        2 * (2 * rows * width + long * width),
        grid=(1,),
        in_specs=[SMEM, whole(rows, width)] + [whole(long, deep)] * 4 + [whole(4 * long, deep)],
        out_specs=whole(count, rows, local_width),
    )(numbers, grads, *own_weights, other_weights)


def weight_gradients(numbers, parts, pieces, units, first=0, blocks=None):
    tokens = parts[0].shape[0]
    chips = len(parts)
    if blocks is None:
        pieces = [piece for chip in pieces for piece in chip]
        long = [p.shape[0] for p in pieces]
    else:
        pieces = [blocks]
        long = [blocks.shape[1]] * 8
    width = pieces[0].shape[-1]
    firsts = [sum(long[:i]) for i in range(len(long))]

    def kernel(numbers_ref, *refs):
        part_refs, piece_refs = refs[:chips], refs[chips : chips + len(pieces)]
        out_ref, buffer, sems = refs[chips + len(pieces) :]

        def source(i):
            return piece_refs[i] if blocks is None else piece_refs[0].at[numbers_ref[0] ^ CHIPS[i]]

        copies = [
            pltpu.make_async_copy(source(i), buffer.at[pl.ds(firsts[i], long[i])], sems.at[i])
            for i in range(len(long))
        ]
        for copy in copies:
            copy.start()
        waited = 0
        for chip in range(chips):
            while waited < len(long) and firsts[waited] < (chip + 1) * tokens:
                copies[waited].wait()
                waited += 1
            rows = buffer[chip * tokens : (chip + 1) * tokens]
            term = product(part_refs[chip][...], rows, COLS_COLS)
            if chip == 0:
                out_ref[...] = term
            else:
                out_ref[...] += term

    return call(
        kernel,
        jax.ShapeDtypeStruct((units, width), jnp.float32),
        2 * chips * tokens * units * width,
        2 * chips * tokens * (units + width) + 4 * units * width,
        grid=(1,),
        in_specs=[SMEM]
        + [pl.BlockSpec((tokens, units), lambda i: (0, first))] * chips
        + [ANY] * len(pieces),
        out_specs=pl.BlockSpec((units, width), lambda i: (0, 0)),
        scratch_shapes=[
            pltpu.VMEM((chips * tokens, width), jnp.bfloat16),
            pltpu.SemaphoreType.DMA((len(long),)),
        ],
    )(numbers, *parts, *pieces)


def eight_plan(
    hidden_in,
    doc_lengths,
    expert_ids,
    fill_rank,
    norm_gains,
    qkv_weight,
    qkv_bias,
    out_weight,
    router_weight,
    blend_weight,
    shared_inner,
    shared_outer,
    expert_inner,
    expert_outer,
    cotangent,
):
    _, tokens, width = hidden_in.shape
    local_width = qkv_weight.shape[2]
    experts = router_weight.shape[1]
    capacity = tokens * TOP // experts
    score_scale = 1.0 / math.sqrt(HEAD_DIM)
    gains = norm_gains.astype(jnp.float32)
    me_tp = lax.axis_index("tp")
    tp = lax.axis_size("tp")
    share = tokens // tp
    number = own_number()
    numbers = jnp.stack([number, me_tp])
    deep = width // 8
    half_width = local_width // 2

    def own_rows(values):
        return lax.dynamic_slice_in_dim(values, me_tp * share, share, axis=0)

    qkv_own = jnp.transpose(qkv_weight, (1, 0, 2))
    qkv_x, qkv_y = swap_x(qkv_own), swap_y(qkv_own)
    qkv_sibling = swap_core(qkv_own)
    out_line = lax.all_gather(out_weight, "tp", axis=0, tiled=True)

    route_rows = expert_ids.reshape(tokens, TOP)
    named = jnp.sum(
        (route_rows[:, :, None] == jnp.arange(experts, dtype=jnp.int32)[None, None, :]).astype(
            jnp.float32
        ),
        axis=1,
    )
    priority = fill_rank.reshape(tokens)
    earlier = (priority[None, :] < priority[:, None]).astype(jnp.bfloat16)
    slot_counts = jnp.dot(
        earlier, named.astype(jnp.bfloat16), preferred_element_type=jnp.float32
    )
    kept_all = named * (slot_counts < capacity).astype(jnp.float32)
    kept_blocks = lax.all_to_all(
        kept_all.T.reshape(experts, 1, tokens),
        ("fsdp", "ctx"),
        split_axis=0,
        concat_axis=0,
        tiled=True,
    )

    positions = lax.axis_index("ctx") * tokens + jnp.arange(tokens, dtype=jnp.int32)
    earlier_pos = positions - tokens
    doc_number, doc_place = document_layout(doc_lengths[0], positions)
    prior_number = document_layout(doc_lengths[0], earlier_pos)[0]
    cosine, sine_table = rotary_tables(doc_place)
    half_dim = HEAD_DIM // 2
    signed_sine = jnp.concatenate([-sine_table[:, :half_dim], sine_table[:, half_dim:]], axis=1)
    masks = []
    for places, doc_numbers in ((positions, doc_number), (earlier_pos, prior_number)):
        distance = positions[:, None] - places[None, :]
        allowed = (
            (distance >= 0)
            & (distance < WINDOW)
            & (places[None, :] >= 0)
            & (doc_number[:, None] == doc_numbers[None, :])
        )
        masks.append(jnp.where(allowed, 0.0, masked_score))

    shared_t = jnp.transpose(shared_inner, (1, 2, 0))
    hid_s = shared_t.shape[1] // 8
    to_trade = jnp.concatenate(
        [
            shared_t.reshape(2, 8, hid_s, deep)[0],
            shared_t.reshape(2, 8, hid_s, deep)[1],
            shared_outer.reshape(8, hid_s, deep),
        ],
        axis=1,
    )

    qkv_x, qkv_y, cosine, signed_sine = after((qkv_x, qkv_y, cosine, signed_sine), kept_all)
    qkv_low = swap_x(qkv_y[:, :, :half_width])
    qkv_high = swap_y(qkv_x[:, :, half_width:])
    qkv_parts = [
        [qkv_own],
        [qkv_y],
        [qkv_sibling],
        [swap_core(qkv_y)],
        [qkv_x],
        [qkv_low, qkv_high],
        [swap_core(qkv_x)],
        [swap_core(qkv_low), swap_core(qkv_high)],
    ]
    hidden_rows = hidden_in.reshape(tokens, width)
    projected, first_normalized = project(
        numbers,
        hidden_rows,
        gains[:1],
        qkv_parts,
        qkv_bias.astype(jnp.float32)[:, None],
        cosine,
        signed_sine,
    )
    prior = from_behind(projected[1:], "ctx", 1)

    out_own = after(out_line, qkv_low, qkv_high)
    out_x, out_y = swap_x(out_own), swap_y(out_own)
    out_both = swap_x(out_y)
    prior = after(prior, out_x, out_both, kept_blocks)
    grad_rows = cotangent.reshape(tokens, width)
    all_grads = lax.all_gather(
        after(grad_rows, prior), ("fsdp", "ctx"), axis=0, tiled=False
    )

    grads_sibling = swap_core(after(grad_rows, projected))

    mixed_result, log_total = attend(projected, prior, masks, score_scale)
    mixed_all = line_gather(mixed_result)

    out_mine = [out_own, out_y, out_x, out_both]
    out_other = swap_core(after(jnp.concatenate(out_mine), mixed_result))
    to_trade = after(to_trade, mixed_result)
    parts_to_trade = exchange_order([to_trade[d] for d in range(8)])
    hidden_rows = hidden_in.reshape(tokens, width)

    trade_arrived = trade_chips(parts_to_trade)
    mixed_all, trade_arrived = after((mixed_all, trade_arrived))
    second_normalized, after_own = attend_out(
        numbers, hidden_rows, gains[1:], mixed_all, out_mine, out_other
    )
    rows_x, rows_y = swap_x(second_normalized), swap_y(second_normalized)
    row_chips = [[swap_core(second_normalized), second_normalized]]
    traded = trade_cores(parts_to_trade, after(trade_arrived, row_chips[0]))

    kept_rel = exchange_order([kept_blocks[i].reshape(tokens, 1) for i in range(8)])
    kept_chips = [jnp.concatenate([kept_rel[p + 2], kept_rel[p]]) for p in (0, 4, 1, 5)]
    shared_rows = jnp.concatenate(exchange_order(after(traded, second_normalized)), axis=1)
    hid_e = expert_inner.shape[3]
    hid = hid_e + hid_s
    router_rows = jnp.concatenate(
        [
            router_weight.T,
            blend_weight[None],
            jnp.zeros((-(experts + 1) % 16, width), jnp.bfloat16),
        ]
    )
    pad = -(-(hid + router_rows.shape[0]) // LANES) * LANES
    inner, outer = lay_weights(
        jnp.transpose(expert_inner[0], (1, 2, 0)),
        expert_outer[0],
        shared_rows,
        router_rows,
        pad,
    )
    mine = (
        jnp.arange(LANES, dtype=jnp.int32) == number + (hid - (pad - LANES))
    ).astype(jnp.float32)[None]
    upstream_own = narrow(numbers, [grads_sibling, grad_rows], CHIPS[:2], outer)

    def mix(chip, *earlier):
        return mixture(
            row_chips[chip],
            upstream if chip else upstream_own,
            max(chip - 1, 0),
            after(kept_chips[chip], earlier),
            mine,
            inner,
            hid_e,
            hid,
            experts,
        )

    half = tokens // 2
    mixes = [mix(0)]
    upstream = narrow(numbers, after(all_grads, mixes[0][0]), CHIPS[2:], outer)
    back_arrived = [swap_core(mixes[0][2])]
    rows_x, rows_y = after((rows_x, rows_y), upstream)
    rows_low = swap_x(rows_y[: tokens // 2])
    rows_high = swap_y(rows_x[tokens // 2 :])
    row_chips += [[swap_core(rows_x), rows_x], [swap_core(rows_y), rows_y]]
    mixes.append(mix(1))
    back_arrived.append(swap_core(mixes[1][2]))
    rows_low, rows_high = after((rows_low, rows_high), mixes[1][0])
    mixes.append(mix(2, back_arrived[0], rows_low, rows_high))
    back_arrived.append(swap_core(mixes[2][2]))
    row_chips.append([swap_core(rows_low), swap_core(rows_high), rows_low, rows_high])
    own_part, x_part = after((mixes[0][3], mixes[1][3]), mixes[2][0])
    x_low_part = add_low(x_part[:half], back_arrived[1][:half])
    x_low = swap_x(x_low_part)
    back_two, x_low_part = after((back_arrived[2], x_low_part))
    y_taken = halves_sum(mixes[2][3], back_two)
    y_high = swap_y(y_taken[1])
    mixes.append(mix(3, y_taken, row_chips[3]))
    back_arrived.append(swap_core(after(mixes[3][2], x_low, y_high)))
    diagonal = halves_sum(mixes[3][3], back_arrived[3])
    hops = [x_low, y_high, swap_x(diagonal[0]), swap_y(diagonal[1])]
    own_part, x_part = after((own_part, x_part), diagonal)
    own_taken = halves_sum(own_part, back_arrived[0])
    x_high_part = add_low(x_part[half:], back_arrived[1][half:])
    taken = [own_taken, (x_low_part, x_high_part), y_taken, diagonal]

    pre_list = [m[0] for m in mixes]
    weighted_list = after([m[1] for m in mixes], taken[3])
    forward = widen(weighted_list, outer)
    hops = after(hops, forward)
    ends = last_hops(last_parts(taken, hops))
    forward = after(forward, hops)
    arrived_forward = [swap_core(forward[2 * chip]) for chip in range(4)]
    forward_taken = [halves_sum(forward[2 * c + 1], arrived_forward[c]) for c in range(4)]
    back_sum = hops_sum(taken, hops, after(ends, forward_taken))
    grad_normed_two = line_reduce(back_sum)
    forward_hops = first_hops(after(forward_taken, back_sum))
    gate_grad = weight_gradients(numbers, after(pre_list, back_sum), row_chips, pad, 0)
    up_grad = weight_gradients(numbers, after(pre_list, gate_grad), row_chips, pad, 1)
    forward_hops = after(forward_hops, up_grad)
    forward_lasts = last_parts(forward_taken, forward_hops)
    grad_normed_two, forward_lasts = after((grad_normed_two, forward_lasts))
    forward_ends = last_hops(forward_lasts)

    grad_y = own_rows(grad_rows).astype(jnp.float32)
    after_norm_grad, gain_two_grad = jax.vjp(root_norm, after_own, gains[1])[1](grad_normed_two)
    grad_after = grad_y + after_norm_grad
    grad_attn = grad_after.astype(jnp.bfloat16)

    grad_heads = attend_out_back(numbers, grad_attn, out_mine, out_other, tp)
    grad_mixed = lax.all_to_all(
        grad_heads, "tp", split_axis=0, concat_axis=0, tiled=True
    ).reshape(tokens, local_width)
    grad_mixed, forward_ends = after((grad_mixed, forward_ends))
    forward_sum = hops_sum(forward_taken, forward_hops, forward_ends)
    grad_mixed, forward_sum = after((grad_mixed, forward_sum))
    grad_query, grad_own, grad_prior = attend_back(
        projected, prior, masks, log_total, grad_mixed, cosine, signed_sine, score_scale
    )
    arrived = from_behind(grad_prior, "ctx", -1)
    layer_own = lax.psum_scatter(forward_sum, "tp", scatter_dimension=0, tiled=True)
    outer_grad = weight_gradients(
        numbers, after(weighted_list, grad_prior), None, pad, 0, all_grads
    )
    layer_own = (after_own + layer_own.astype(jnp.float32)).astype(jnp.bfloat16)
    heads_own = after(
        lax.dynamic_slice_in_dim(mixed_all, me_tp * share, share, axis=1), outer_grad
    )
    projection_full = lax.dot_general(
        heads_own, grad_attn, (((1,), (0,)), ((), ())), preferred_element_type=jnp.float32
    ).astype(jnp.bfloat16)
    arrived, outer_grad, layer_own = after((arrived, outer_grad, layer_own))
    projection_grad = lax.psum_scatter(
        after(projection_full, arrived).reshape(tp * local_width, width),
        ("fsdp", "ctx"),
        scatter_dimension=1,
        tiled=True,
    )
    grad_linear, bias_part, gain_one_part, grad_one_part = project_back(
        numbers, grad_query, grad_own, arrived, cosine, signed_sine, hidden_rows, qkv_parts
    )
    layer_out = hop_gather(layer_own).reshape(1, tokens, width)
    grad_normed_one = lax.psum_scatter(
        grad_one_part, "tp", scatter_dimension=0, tiled=True
    ).astype(jnp.float32)
    first = grad_one_part
    gate_grad, up_grad, outer_grad = after((gate_grad, up_grad, outer_grad), first)
    inner_expert = jnp.transpose(jnp.stack([gate_grad[:hid_e], up_grad[:hid_e]]), (2, 0, 1))[None]
    outer_expert = outer_grad[:hid_e][None]
    shared_grad = jnp.concatenate(
        [gate_grad[hid_e:hid], up_grad[hid_e:hid], outer_grad[hid_e:hid]]
    ).astype(jnp.bfloat16)
    shared_parts = exchange_order(columns_of(shared_grad, 8))

    small = sum_eight(
        jnp.concatenate(
            [
                gate_grad[hid : hid + experts + 1],
                after(gain_one_part, first),
                gain_two_grad[None],
                jnp.pad(
                    after(bias_part, first).reshape(1, 3 * local_width),
                    ((0, 0), (0, width - 3 * local_width)),
                ),
            ]
        )
    )
    bias_grad = small[experts + 3, : 3 * local_width].reshape(3, local_width)
    small = small[: experts + 3]
    shared_parts = after(shared_parts, small)
    shared_parts = trade_cores(shared_parts, trade_chips(shared_parts))
    shared_back = jnp.stack(exchange_order(shared_parts))
    inner_shared = jnp.transpose(
        jnp.stack([shared_back[:, :hid_s], shared_back[:, hid_s : 2 * hid_s]]).reshape(
            2, 8 * hid_s, deep
        ),
        (2, 0, 1),
    ).astype(jnp.float32)
    outer_shared = shared_back[:, 2 * hid_s :].reshape(8 * hid_s, deep).astype(jnp.float32)
    qkv_full = project_weights(first_normalized, after(grad_linear, grad_one_part))
    qkv_arrived = lax.all_to_all(
        after(qkv_full, small), ("fsdp", "ctx"), split_axis=0, concat_axis=0, tiled=True
    )
    qkv_grad = jnp.transpose(jnp.sum(qkv_arrived.astype(jnp.float32), axis=0), (1, 0, 2))

    residual_own = own_rows(hidden_rows).astype(jnp.float32)
    residual_norm_grad, _ = jax.vjp(root_norm, residual_own, gains[0])[1](grad_normed_one)
    input_own = (grad_after + residual_norm_grad).astype(jnp.bfloat16)
    small = sum_line(small)
    input_own, layer_out, inner_shared, outer_shared, inner_expert, small = after(
        (input_own, layer_out, inner_shared, outer_shared, inner_expert, small)
    )
    input_grad = hop_gather(input_own).reshape(1, tokens, width)
    projection_grad = lax.psum_scatter(
        projection_grad, "tp", scatter_dimension=0, tiled=True
    ).astype(jnp.float32)
    router_grad = small[:experts].T
    blend_grad = small[experts]
    gains_grad = small[experts + 1 :]
    return (
        layer_out,
        input_grad,
        gains_grad,
        qkv_grad,
        bias_grad,
        projection_grad,
        router_grad,
        blend_grad,
        inner_shared,
        outer_shared,
        inner_expert,
        outer_expert,
    )


def solution(mesh):
    placed = (
        P("fsdp", "ctx", None),
        P("fsdp", None),
        P("fsdp", "ctx", None),
        P("fsdp", "ctx", None),
        P(),
        P(("fsdp", "ctx"), None, "tp"),
        P(None, "tp"),
        P("tp", ("fsdp", "ctx")),
        P(),
        P(),
        P(("fsdp", "ctx"), None, "tp"),
        P("tp", ("fsdp", "ctx")),
        P(("fsdp", "ctx"), None, None, "tp"),
        P(("fsdp", "ctx"), "tp", None),
        P("fsdp", "ctx", None),
    )
    plan = eight_plan if mesh.shape["fsdp"] == 4 and mesh.shape["ctx"] == 2 else general_plan
    return jax.shard_map(
        plan,
        mesh=mesh,
        in_specs=placed,
        out_specs=(
            P("fsdp", "ctx", None),
            P("fsdp", "ctx", None),
            P(),
            P(("fsdp", "ctx"), None, "tp"),
            P(None, "tp"),
            P("tp", ("fsdp", "ctx")),
            P(),
            P(),
            P(("fsdp", "ctx"), None, "tp"),
            P("tp", ("fsdp", "ctx")),
            P(("fsdp", "ctx"), None, None, "tp"),
            P(("fsdp", "ctx"), "tp", None),
        ),
        check_vma=False,
    )
```
